32 devices in a mesh: section: 2 (over x), ctx: 4 (over y, core), wt: 4 (over z).
Axes of the slice: x: 2, y: 2, z: 4, core: 2. Of those that a mesh axis runs over, the one named last changes fastest.
Arguments:
- feed: bfloat16 [2, 2, 4, 1024, 1600], P('section', None, 'wt', 'ctx'), may hold values from -6 to 6
- block_order: int32 [8], replicated, may hold values from 0 to 7, as said below
- attn_gain: bfloat16 [2, 1600], P('section', 'wt'), may hold values from 0.5 to 1.5
- attn_shift: bfloat16 [2, 1600], P('section', 'wt'), may hold values from -3 to 3
- w_qkv: bfloat16 [2, 1600, 4800], P('section', 'wt'), may hold values from -0.15625 to 0.15625
- query_bias: bfloat16 [2, 1600], P('section', 'wt'), may hold values from -3 to 3
- value_bias: bfloat16 [2, 1600], P('section', 'wt'), may hold values from -3 to 3
- w_proj: bfloat16 [2, 1600, 1600], P('section', 'wt'), may hold values from -1.75 to 1.75
- proj_bias: bfloat16 [2, 1600], P('section', 'wt'), may hold values from -3 to 3
- mlp_gain: bfloat16 [2, 1600], P('section', 'wt'), may hold values from 0.5 to 1.5
- mlp_shift: bfloat16 [2, 1600], P('section', 'wt'), may hold values from -3 to 3
- w_fc: bfloat16 [2, 1600, 6400], P('section', 'wt'), may hold values from -0.15625 to 0.15625
- fc_bias: bfloat16 [2, 6400], P('section', 'wt'), may hold values from -3 to 3
- w_out: bfloat16 [2, 6400, 1600], P('section', 'wt'), may hold values from -0.078125 to 0.078125
- out_bias: bfloat16 [2, 1600], P('section', 'wt'), may hold values from -3 to 3
Outputs:
- result: bfloat16 [2, 2, 4, 1024, 1600], P('section', None, 'wt', 'ctx')
- attn_gain_grad: float32 [2, 1600], P('section', 'wt')
- attn_shift_grad: float32 [2, 1600], P('section', 'wt')
- w_qkv_grad: float32 [2, 1600, 4800], P('section', 'wt')
- query_bias_grad: float32 [2, 1600], P('section', 'wt')
- value_bias_grad: float32 [2, 1600], P('section', 'wt')
- w_proj_grad: float32 [2, 1600, 1600], P('section', 'wt')
- proj_bias_grad: float32 [2, 1600], P('section', 'wt')
- mlp_gain_grad: float32 [2, 1600], P('section', 'wt')
- mlp_shift_grad: float32 [2, 1600], P('section', 'wt')
- w_fc_grad: float32 [2, 1600, 6400], P('section', 'wt')
- fc_bias_grad: float32 [2, 6400], P('section', 'wt')
- w_out_grad: float32 [2, 6400, 1600], P('section', 'wt')
- out_bias_grad: float32 [2, 1600], P('section', 'wt')
The draws below stay inside these ranges and needn't reach their ends.
Inputs may be any that keep to these rules, and one draw needn't show every extreme that they name: `block_order`: A permutation of the 8 blocks of a sequence, the same for every sequence: entry t names the block stored in slot t; slots 2 * c and 2 * c + 1 hold blocks b and 7 - b for some b.
All inputs are finite; a program needn't handle non-finite values.
Results may differ from the reference program's by a relative error of at most 0.017.
Values may be sent and summed in bfloat16 or wider, within the bound.
No kernel may reach another device: no remote copies, remote signals or barrier semaphores. Data moves between devices by JAX's collectives and lax.ppermute only.
A program may use at most 512 MiB of HBM per device.

```python
import math
import jax
import jax.numpy as jnp
from jax import lax

HEADS = 25
HEAD_DIM = 64
D = 1600
FF = 6400
LENGTH = 1024
MICRO = 2
SEQS = 4
NBLK = 8
BLK = 128


def draw_block_order(key, part):
    key = jax.random.fold_in(key, 3)
    first_key, second_key = jax.random.split(key)
    halves = NBLK // 2
    chosen = jax.random.permutation(first_key, halves).astype(jnp.int32)
    flipped = jax.random.randint(second_key, (halves,), 0, 2).astype(jnp.int32)
    mirrored = (NBLK - 1 - chosen).astype(jnp.int32)
    leading = jnp.where(flipped == 1, mirrored, chosen)
    trailing = jnp.where(flipped == 1, chosen, mirrored)
    return jnp.stack([leading, trailing], 1).reshape(NBLK).astype(jnp.int32)


def block_levels(rng, extent, shards, least, high):
    def one(dim, shards_of):
        heights = jax.random.uniform(jax.random.fold_in(jax.random.fold_in(rng, 6), dim), (shards_of,), jnp.float32, least / len(shards), high / len(shards))
        return jnp.repeat(jnp.exp(heights), extent[dim] // shards_of).reshape((-1,) + (1,) * (len(extent) - dim - 1))

    factor_of = one(*shards[0])
    for cut in shards[1:]:
        factor_of = factor_of * one(*cut)
    return factor_of


def gaussian(stream_key, extent, width, bound, cuts=(), held_as=jnp.bfloat16):
    entries = jax.random.normal(stream_key, extent, jnp.float32) * width
    if len(cuts) > 0:
        entries = block_levels(stream_key, extent, cuts, -0.22, 0.18) * entries
    return jnp.clip(entries, min=-bound, max=bound).astype(held_as)


def setup_inputs(seed: int = 0) -> dict:
    splits = jax.random.split(jax.random.key(seed), 16)
    return {
        "feed": gaussian(splits[0], (2, MICRO, SEQS, LENGTH, D), 1.0, 6.0, ((0, 2), (2, 4), (3, 4))),
        "block_order": draw_block_order(jax.random.fold_in(splits[15], 71), 0),
        "attn_gain": jnp.clip(1.0 + 0.1 * jax.random.normal(splits[2], (2, D), jnp.float32), 0.5, 1.5).astype(jnp.bfloat16),
        "attn_shift": gaussian(splits[3], (2, D), 0.5, 3.0, ((0, 2), (1, 4))),
        "w_qkv": gaussian(splits[4], (2, D, 3 * D), D ** -0.5, 0.15625, ((0, 2), (1, 4))),
        "query_bias": gaussian(splits[5], (2, D), 0.5, 3.0, ((0, 2), (1, 4))),
        "value_bias": gaussian(splits[6], (2, D), 0.5, 3.0, ((0, 2), (1, 4))),
        "w_proj": gaussian(splits[7], (2, D, D), (max(D // 128, 4)) ** -0.5, 1.75, ((0, 2), (1, 4))),
        "proj_bias": gaussian(splits[8], (2, D), 0.5, 3.0, ((0, 2), (1, 4))),
        "mlp_gain": jnp.clip(1.0 + 0.1 * jax.random.normal(splits[9], (2, D), jnp.float32), 0.5, 1.5).astype(jnp.bfloat16),
        "mlp_shift": gaussian(splits[10], (2, D), 0.5, 3.0, ((0, 2), (1, 4))),
        "w_fc": gaussian(splits[11], (2, D, FF), D ** -0.5, 0.15625, ((0, 2), (1, 4))),
        "fc_bias": gaussian(splits[12], (2, FF), 0.5, 3.0, ((0, 2), (1, 4))),
        "w_out": gaussian(splits[13], (2, FF, D), FF ** -0.5, 0.078125, ((0, 2), (1, 4))),
        "out_bias": gaussian(splits[14], (2, D), 0.5, 3.0, ((0, 2), (1, 4))),
    }


@jax.custom_vjp
def low(v):
    return lax.optimization_barrier(v.astype(jnp.bfloat16)).astype(jnp.float32)

@jax.custom_vjp
def low_back(v):
    return v

def low_keep(v):
    return (low(v), None)

def low_pass(kept, grad):
    return (grad,)

def back_keep(v):
    return (v, None)

def back_low(kept, grad):
    return (low(grad),)
low.defvjp(low_keep, low_pass)
low_back.defvjp(back_keep, back_low)
EPS = 1e-05
NEG = -1000000000.0
HIGH = lax.Precision.HIGHEST

def rounded_both(values):
    return low_back(low(values))

def dense(left, right):
    return jnp.dot(left, right, precision=HIGH, preferred_element_type=jnp.float32)

def layer_norm(values):
    center = values - lax.optimization_barrier(jnp.mean(values, -1, keepdims=True))
    spread = lax.optimization_barrier(jnp.mean(center * center, -1, keepdims=True))
    return center * lax.rsqrt(spread + EPS)

def attention(query, keyed, valued, position):
    qblock = math.gcd(LENGTH, 512)
    count = LENGTH // qblock
    scale = HEAD_DIM ** (-0.5)
    keys_h = keyed.reshape(LENGTH, HEADS, HEAD_DIM)
    values_h = valued.reshape(LENGTH, HEADS, HEAD_DIM)

    def block(inputs):
        query_part, place = inputs
        scores = jnp.einsum('qhd,khd->hqk', query_part.reshape(qblock, HEADS, HEAD_DIM), keys_h, precision=HIGH) * scale
        scores = low_back(scores)
        allowed = position[None, :] <= place[:, None]
        scores = jnp.where(allowed[None], scores, NEG)
        chance = low(jax.nn.softmax(scores, axis=-1))
        mixed = jnp.einsum('hqk,khd->qhd', chance, values_h, precision=HIGH)
        return mixed.reshape(qblock, HEADS * HEAD_DIM)
    outputs = lax.map(jax.checkpoint(block), (query.reshape(count, qblock, D), position.reshape(count, qblock)))
    return outputs.reshape(LENGTH, D)

def layer(stream, params, position):
    attn_gain, attn_shift, w_qkv, query_bias, value_bias, w_proj, proj_bias, mlp_gain, mlp_shift, w_fc, fc_bias, w_out, out_bias = params
    normed = low(layer_norm(stream) * attn_gain + attn_shift)
    project = dense(normed, w_qkv)
    query = rounded_both(project[:, :D] + query_bias)
    keyed = rounded_both(project[:, D:2 * D])
    valued = rounded_both(project[:, 2 * D:] + value_bias)
    mixed = rounded_both(attention(query, keyed, valued, position))
    middle = stream + low_back(dense(mixed, w_proj) + proj_bias)
    second = low(layer_norm(middle) * mlp_gain + mlp_shift)
    hidden = low_back(dense(second, w_fc) + fc_bias)
    active = low(jax.nn.gelu(hidden, approximate=True))
    return middle + low_back(dense(active, w_out) + out_bias)

def reference(feed, block_order, attn_gain, attn_shift, w_qkv, query_bias, value_bias, w_proj, proj_bias, mlp_gain, mlp_shift, w_fc, fc_bias, w_out, out_bias):
    offsets = jnp.arange(LENGTH, dtype=jnp.int32)
    position = (block_order[(offsets // BLK).astype(jnp.int32)] * BLK + offsets % BLK).astype(jnp.int32)
    inputs = feed[0].astype(jnp.float32).reshape(MICRO * SEQS, LENGTH, D)
    cotangent = feed[1].astype(jnp.float32).reshape(MICRO * SEQS, LENGTH, D)
    weights = tuple((piece.astype(jnp.float32) for piece in (attn_gain, attn_shift, w_qkv, query_bias, value_bias, w_proj, proj_bias, mlp_gain, mlp_shift, w_fc, fc_bias, w_out, out_bias)))

    def forward(streams, params):
        first = tuple((piece[0] for piece in params))
        second = tuple((piece[1] for piece in params))

        def sequence(stream):
            return layer(rounded_both(layer(stream, first, position)), second, position)
        return lax.map(jax.checkpoint(sequence), streams)
    outputs, pullback = jax.vjp(forward, inputs, weights)
    grad_inputs, grads = pullback(cotangent)
    result = jnp.stack([grad_inputs, outputs]).reshape(2, MICRO, SEQS, LENGTH, D).astype(jnp.bfloat16)
    return (result, grads[0], grads[1], grads[2], grads[3], grads[4], grads[5], grads[6], grads[7], grads[8], grads[9], grads[10], grads[11], grads[12])
```

```python
import functools
import math

import jax
import jax.numpy as jnp
from jax import lax
from jax.experimental import pallas as pl
from jax.experimental.pallas import tpu as pltpu
from jax.sharding import PartitionSpec as P

HEAD_DIM = 64
NEG = -1000000000.0
LANES = 128


def nt_dot(left, right):
    return lax.dot_general(left, right, (((1,), (1,)), ((), ())), preferred_element_type=jnp.float32)


def nn_dot(left, right):
    return jnp.dot(left, right, preferred_element_type=jnp.float32)


def causal_scores(keys, query, tile):
    scores = nt_dot(keys, query)
    edge = scores.shape[0] - tile
    key_at = lax.broadcasted_iota(jnp.int32, (tile, tile), 0)
    query_at = lax.broadcasted_iota(jnp.int32, (tile, tile), 1)
    last = jnp.where(key_at <= query_at, scores[edge:], NEG)
    return jnp.concatenate([scores[:edge], last], 0) if edge else last


def attend_kernel(block, tile, heads, place, qkv, out, log_total, query, keyed, valued, mixed):
    length, three = qkv.shape
    span = three // 3
    lane = lax.broadcasted_iota(jnp.int32, (tile, LANES), 1)

    def pair(index, carry):
        start = pl.multiple_of(index * LANES, LANES)
        for at in range(length // block):
            rows = pl.ds(pl.multiple_of(place[at] * block, block), block)
            here = pl.ds(at * block, block)
            query[here, :] = qkv[rows, pl.ds(start, LANES)] * (HEAD_DIM ** (-0.5))
            keyed[here, :] = qkv[rows, pl.ds(span + start, LANES)]
            valued[:, here] = qkv[rows, pl.ds(2 * span + start, LANES)].T

        for half in range(2):

            @pl.when(2 * index + half < heads)
            def _():
                mine = (lane < HEAD_DIM) if half == 0 else (lane >= HEAD_DIM)
                features = slice(half * HEAD_DIM, (half + 1) * HEAD_DIM)
                for at in range(length // tile):
                    seen = (at + 1) * tile
                    cols = slice(at * tile, seen)
                    part = jnp.where(mine, query[cols, :], 0)
                    scores = causal_scores(keyed[:seen, :], part, tile)
                    highest = jnp.max(scores, 0, keepdims=True)
                    exponent = jnp.exp(scores - highest)
                    total = jnp.sum(exponent, 0, keepdims=True)
                    result = nn_dot(valued[features, :seen], exponent.astype(jnp.bfloat16))
                    mixed[features, cols] = result * (1.0 / total)
                    log_total[pl.ds(2 * index + half, 1), cols] = highest + jnp.log(total)

        for at in range(length // block):
            rows = pl.ds(pl.multiple_of(place[at] * block, block), block)
            out[rows, pl.ds(start, LANES)] = mixed[:, at * block : (at + 1) * block].T.astype(out.dtype)
        return carry

    mixed[...] = jnp.zeros_like(mixed)
    lax.fori_loop(0, span // LANES, pair, 0)


def attend(place, qkv, heads, block):
    length, three = qkv.shape
    span = three // 3
    tile = min(256, length)
    rows = -(-span // HEAD_DIM // 8) * 8
    vmem = pl.BlockSpec(memory_space=pltpu.VMEM)
    return pl.pallas_call(
        functools.partial(attend_kernel, block, tile, heads),
        out_shape=(
            jax.ShapeDtypeStruct((length, span), jnp.bfloat16),
            jax.ShapeDtypeStruct((rows, length), jnp.float32),
        ),
        in_specs=[pl.BlockSpec(memory_space=pltpu.SMEM), vmem],
        out_specs=(vmem, vmem),
        scratch_shapes=[
            pltpu.VMEM((length, LANES), jnp.bfloat16),
            pltpu.VMEM((length, LANES), jnp.bfloat16),
            pltpu.VMEM((LANES, length), jnp.bfloat16),
            pltpu.VMEM((LANES, length), jnp.float32),
        ],
        compiler_params=pltpu.CompilerParams(vmem_limit_bytes=40 * 1024 * 1024),
        cost_estimate=pl.CostEstimate(
            flops=3 * heads * length * length * HEAD_DIM,
            bytes_accessed=2 * length * 4 * span,
            transcendentals=heads * length * length // 2,
        ),
    )(place, qkv)


def attend_back_kernel(
    block, tile, heads, place, qkv, grad_mixed, log_total, out,
    query, keyed, keyed_t, valued, grad, grad_query, grad_key, grad_value,
):
    length, three = qkv.shape
    span = three // 3
    scale = HEAD_DIM ** (-0.5)
    lane = lax.broadcasted_iota(jnp.int32, (tile, LANES), 1)

    def pair(index, carry):
        start = pl.multiple_of(index * LANES, LANES)
        for at in range(length // block):
            rows = pl.ds(pl.multiple_of(place[at] * block, block), block)
            here = pl.ds(at * block, block)
            query[here, :] = qkv[rows, pl.ds(start, LANES)] * scale
            key_part = qkv[rows, pl.ds(span + start, LANES)]
            keyed[here, :] = key_part
            keyed_t[:, here] = key_part.T
            valued[here, :] = qkv[rows, pl.ds(2 * span + start, LANES)]
            grad[here, :] = grad_mixed[rows, pl.ds(start, LANES)]
        grad_query[...] = jnp.zeros_like(grad_query)
        grad_key[...] = jnp.zeros_like(grad_key)
        grad_value[...] = jnp.zeros_like(grad_value)

        for half in range(2):

            @pl.when(2 * index + half < heads)
            def _():
                mine = (lane < HEAD_DIM) if half == 0 else (lane >= HEAD_DIM)
                features = slice(half * HEAD_DIM, (half + 1) * HEAD_DIM)
                for at in range(length // tile):
                    seen = (at + 1) * tile
                    cols = slice(at * tile, seen)
                    part = jnp.where(mine, query[cols, :], 0)
                    grad_part = jnp.where(mine, grad[cols, :], 0)
                    scores = causal_scores(keyed[:seen, :], part, tile)
                    chance = jnp.exp(scores - log_total[pl.ds(2 * index + half, 1), cols])
                    grad_chance = nt_dot(valued[:seen, :], grad_part)
                    inner = jnp.sum(chance * grad_chance, 0, keepdims=True)
                    grad_scores = (chance * (grad_chance - inner)).astype(jnp.bfloat16)
                    grad_value[:seen, :] += nn_dot(chance.astype(jnp.bfloat16), grad_part)
                    grad_key[:seen, :] += nn_dot(grad_scores, part)
                    grad_query[features, cols] = nn_dot(keyed_t[features, :seen], grad_scores) * scale

        for at in range(length // block):
            rows = pl.ds(pl.multiple_of(place[at] * block, block), block)
            here = slice(at * block, (at + 1) * block)
            out[rows, pl.ds(start, LANES)] = grad_query[:, here].T.astype(out.dtype)
            out[rows, pl.ds(span + start, LANES)] = grad_key[here, :].astype(out.dtype)
            out[rows, pl.ds(2 * span + start, LANES)] = grad_value[here, :].astype(out.dtype)
        return carry

    lax.fori_loop(0, span // LANES, pair, 0)


def attend_back(place, qkv, grad_mixed, log_total, heads, block):
    length, three = qkv.shape
    span = three // 3
    tile = min(256, length)
    vmem = pl.BlockSpec(memory_space=pltpu.VMEM)
    return pl.pallas_call(
        functools.partial(attend_back_kernel, block, tile, heads),
        out_shape=jax.ShapeDtypeStruct((length, three), jnp.bfloat16),
        in_specs=[pl.BlockSpec(memory_space=pltpu.SMEM), vmem, vmem, vmem],
        out_specs=vmem,
        scratch_shapes=[
            pltpu.VMEM((length, LANES), jnp.bfloat16),
            pltpu.VMEM((length, LANES), jnp.bfloat16),
            pltpu.VMEM((LANES, length), jnp.bfloat16),
            pltpu.VMEM((length, LANES), jnp.bfloat16),
            pltpu.VMEM((length, LANES), jnp.bfloat16),
            pltpu.VMEM((LANES, length), jnp.float32),
            pltpu.VMEM((length, LANES), jnp.float32),
            pltpu.VMEM((length, LANES), jnp.float32),
        ],
        compiler_params=pltpu.CompilerParams(vmem_limit_bytes=48 * 1024 * 1024),
        cost_estimate=pl.CostEstimate(
            flops=7 * heads * length * length * HEAD_DIM,
            bytes_accessed=2 * length * 7 * span,
            transcendentals=heads * length * length // 2,
        ),
    )(place, qkv, grad_mixed, log_total)


EPS = 1e-05
GELU_A = math.sqrt(2.0 / math.pi)
GELU_B = 0.044715


def flip(axis, bit):
    return [(at, at ^ bit) for at in range(lax.axis_size(axis))]


def swap(value, axis, bit=1):
    return lax.ppermute(value, axis, flip(axis, bit))


def bits_of(axis):
    bits, bit = [], 1
    while bit < lax.axis_size(axis):
        bits.append(bit)
        bit *= 2
    return bits


def gathered(value, axis):
    pieces = {0: value}
    for bit in reversed(bits_of(axis)):
        for at in list(pieces):
            pieces[at | bit] = swap(pieces[at], axis, bit)
    return [pieces[at] for at in range(lax.axis_size(axis))]


def summed(pieces, axis):
    pieces = dict(enumerate(pieces))
    for bit in bits_of(axis):
        for at in sorted(pieces, reverse=True):
            if at & bit:
                came = swap(pieces.pop(at).astype(jnp.bfloat16), axis, bit)
                pieces[at ^ bit] = pieces[at ^ bit].astype(jnp.float32) + came.astype(jnp.float32)
    return pieces[0]


def exchanged(pieces, axis):
    return [swap(piece, axis, at) if at else piece for at, piece in enumerate(pieces)]


def by_owner(pieces, axis):
    here = lax.axis_index(axis)
    whole = jnp.zeros((len(pieces),) + pieces[0].shape, pieces[0].dtype)
    for at, piece in enumerate(pieces):
        whole = lax.dynamic_update_index_in_dim(whole, piece, here ^ at, 0)
    return whole


def over_wt(value, tiled=True):
    return lax.all_gather(value, "wt", axis=0, tiled=tiled)


def scatter_wt(value, tiled=True):
    return lax.psum_scatter(value, "wt", scatter_dimension=0, tiled=tiled)


def dot(left, right):
    return jnp.dot(left, right, preferred_element_type=jnp.float32)


def dot_nt(left, right):
    return lax.dot_general(left, right, (((1,), (1,)), ((), ())), preferred_element_type=jnp.float32)


def dot_tn(left, right):
    return lax.dot_general(left, right, (((0,), (0,)), ((), ())), preferred_element_type=jnp.float32)


def low(value):
    return value.astype(jnp.bfloat16)


def wide(value):
    return value.astype(jnp.float32)


def normed(values):
    center = values - jnp.mean(values, -1, keepdims=True)
    rate = lax.rsqrt(jnp.mean(center * center, -1, keepdims=True) + EPS)
    return center * rate, rate


def norm_back(grad, gain, values):
    unit, rate = normed(values)
    inner = grad * gain
    back = rate * (
        inner
        - jnp.mean(inner, -1, keepdims=True)
        - unit * jnp.mean(inner * unit, -1, keepdims=True)
    )
    return back, jnp.sum(grad * unit, 0), jnp.sum(grad, 0)


def gelu(value):
    return 0.5 * value * (1.0 + jnp.tanh(GELU_A * (value + GELU_B * value * value * value)))


def gelu_slope(value):
    square = value * value
    bend = jnp.tanh(GELU_A * (value + GELU_B * value * square))
    return 0.5 * (1.0 + bend) + 0.5 * value * (1.0 - bend * bend) * (
        GELU_A * (1.0 + 3.0 * GELU_B * square)
    )


class Plan:
    def __init__(self, width, hidden_rows):
        self.count = lax.axis_size("ctx")
        self.ci = lax.axis_index("ctx")
        self.first = lax.axis_index("section") == 0
        self.xi = lax.axis_index("section")
        self.wi = lax.axis_index("wt")
        self.width = width
        heads = width // HEAD_DIM
        stride = heads // self.count
        self.heads = heads - stride * (self.count - 1)
        self.step = stride * HEAD_DIM
        self.span = (self.heads + self.heads % 2) * HEAD_DIM
        self.padded = self.step * (self.count - 1) + self.span
        self.owned = jnp.where(self.ci == self.count - 1, self.heads, stride) * HEAD_DIM
        self.part = hidden_rows // self.count
        self.half = self.part // 2

    def padded_out(self, array):
        return jnp.pad(array, [(0, 0)] * (array.ndim - 1) + [(0, self.padded - array.shape[-1])])

    def window(self, padded, index):
        return lax.dynamic_slice_in_dim(padded, index * self.step, self.span, padded.ndim - 1)

    def joined(self, ordered):
        last = self.width - self.step * (self.count - 1)
        parts = [ordered[at, ..., : self.step] for at in range(self.count - 1)]
        return jnp.concatenate(parts + [ordered[self.count - 1, ..., :last]], -1)


def forward_layer(entering, weights, vectors, plan, place, block):
    w_qkv, w_proj, w_fc, w_out = weights
    attn_gain, attn_shift, bias_qkv, proj_bias, mlp_gain, mlp_shift, fc_bias, out_bias = vectors
    stream = wide(entering)
    first_norm = jnp.concatenate(gathered(low(normed(stream)[0] * attn_gain + attn_shift), "ctx"))
    qkv = low(dot(first_norm, w_qkv) + bias_qkv)
    mixed, log_total = attend(place, qkv, plan.heads, block)
    rows = entering.shape[0]
    pieces = [mixed[at * rows : (at + 1) * rows] for at in range(plan.count)]
    mixed_all = plan.joined(by_owner(exchanged(pieces, "ctx"), "ctx"))
    middle = stream + (dot(mixed_all, w_proj) + proj_bias)
    second_norm = jnp.concatenate(gathered(low(normed(middle)[0] * mlp_gain + mlp_shift), "ctx"))
    hidden = [dot(second_norm, part) + bias for part, bias in zip(w_fc, fc_bias)]
    active = [low(gelu(part)) for part in hidden]
    result = dot(active[0], w_out[0]) + dot(active[1], w_out[1])
    pieces = [result[at * rows : (at + 1) * rows] for at in range(plan.count)]
    final = middle + (summed(pieces, "ctx") + out_bias)
    kept = (stream, first_norm, qkv, log_total, mixed_all, middle, second_norm, hidden, active)
    return low(final), kept


def backward_layer(coming, kept, weights, vectors, plan, place, block):
    w_qkv, w_proj, w_fc, w_out = weights
    attn_gain, attn_shift, bias_qkv, proj_bias, mlp_gain, mlp_shift, fc_bias, out_bias = vectors
    stream, first_norm, qkv, log_total, mixed_all, middle, second_norm, hidden, active = kept
    rows = coming.shape[0]
    grad_final = wide(coming)
    g_out_bias = jnp.sum(grad_final, 0)
    coming_all = jnp.concatenate(gathered(coming, "ctx"))
    grad_hidden = [
        low(dot_nt(coming_all, part) * gelu_slope(at)) for part, at in zip(w_out, hidden)
    ]
    g_w_out = [low(dot_tn(part, coming_all)) for part in active]
    g_fc_bias = [jnp.sum(wide(part), 0) for part in grad_hidden]
    g_w_fc = [low(dot_tn(second_norm, part)) for part in grad_hidden]
    grad_second = dot_nt(grad_hidden[0], w_fc[0]) + dot_nt(grad_hidden[1], w_fc[1])
    pieces = [grad_second[at * rows : (at + 1) * rows] for at in range(plan.count)]
    back, g_mlp_gain, g_mlp_shift = norm_back(summed(pieces, "ctx"), mlp_gain, middle)
    grad_middle = grad_final + back
    branch = low(grad_middle)
    g_proj_bias = jnp.sum(wide(branch), 0)
    grad_mixed = plan.padded_out(low(dot_nt(branch, w_proj)))
    pieces = [plan.window(grad_mixed, plan.ci ^ at) for at in range(plan.count)]
    g_w_proj = low(dot_tn(mixed_all, branch))
    grad_heads = jnp.concatenate(exchanged(pieces, "ctx"))
    column = lax.broadcasted_iota(jnp.int32, grad_heads.shape, 1)
    grad_heads = jnp.where(column < plan.owned, grad_heads, 0)
    grad_qkv = attend_back(place, qkv, grad_heads, log_total, plan.heads, block)
    g_bias_qkv = jnp.sum(wide(grad_qkv), 0)
    g_w_qkv = low(dot_tn(first_norm, grad_qkv))
    grad_first = dot_nt(grad_qkv, w_qkv)
    pieces = [grad_first[at * rows : (at + 1) * rows] for at in range(plan.count)]
    back, g_attn_gain, g_attn_shift = norm_back(summed(pieces, "ctx"), attn_gain, stream)
    vectors_grad = (
        g_attn_gain,
        g_attn_shift,
        g_bias_qkv,
        g_proj_bias,
        g_mlp_gain,
        g_mlp_shift,
        g_fc_bias,
        g_out_bias,
    )
    return low(grad_middle + back), (g_w_qkv, g_w_proj, g_w_fc, g_w_out), vectors_grad


def body(
    feed,
    block_order,
    attn_gain,
    attn_shift,
    w_qkv,
    query_bias,
    value_bias,
    w_proj,
    proj_bias,
    mlp_gain,
    mlp_shift,
    w_fc,
    fc_bias,
    w_out,
    out_bias,
):
    width = w_proj.shape[2]
    shard = w_proj.shape[1]
    hidden_rows = w_out.shape[1]
    plan = Plan(width, hidden_rows)
    count, owners = plan.count, lax.axis_size("wt")
    first, xi, ci = plan.first, plan.xi, plan.ci
    part, half, span = plan.part, plan.half, plan.span
    rows = feed.shape[3]
    block = rows // 2

    def mine_other(mine, other):
        return (jnp.where(first, mine, other), jnp.where(first, other, mine))

    slots = jnp.arange(2 * count, dtype=jnp.int32)
    held = 2 * (ci ^ (slots // 2)) + slots % 2
    table = (held[:, None] == slots[None, :]).astype(jnp.int32)
    blocks_held = jnp.sum(table * block_order[None, :], 1)
    found = (blocks_held[None, :] == slots[:, None]).astype(jnp.int32)
    place = jnp.sum(found * slots[None, :], 1)

    local = feed[0, :, 0]
    own = lax.dynamic_index_in_dim(local, xi, 0, keepdims=False)
    came = swap(lax.dynamic_index_in_dim(local, 1 - xi, 0, keepdims=False), "section")
    entering, coming = mine_other(own, came)

    fc_part = lax.dynamic_slice_in_dim(fc_bias[0], ci * part, part, 0)
    small = jnp.concatenate(
        [
            vector[0]
            for vector in (
                attn_gain, attn_shift, query_bias, value_bias, proj_bias, mlp_gain, mlp_shift, out_bias
            )
        ]
        + [fc_part]
    )
    small = wide(lax.all_gather(small, ("section", "wt"))).reshape(2, owners, small.shape[0])

    def vectors_of(layer):
        full = jnp.swapaxes(small[layer, :, : 8 * shard].reshape(owners, 8, shard), 0, 1)
        full = full.reshape(8, owners * shard)
        hidden = small[layer, :, 8 * shard :]
        halves = [
            lax.dynamic_slice_in_dim(hidden, duty * half, half, 1).reshape(-1) for duty in (xi, 1 - xi)
        ]
        query = plan.window(plan.padded_out(full[2]), ci)
        value = plan.window(plan.padded_out(full[3]), ci)
        bias_qkv = jnp.concatenate([query, jnp.zeros_like(query), value])
        return (full[0], full[1], bias_qkv, full[4], full[5], full[6], halves, full[7])

    qkv_shard = jnp.concatenate(
        [
            plan.window(plan.padded_out(w_qkv[0][:, at * width : (at + 1) * width]), ci)
            for at in range(3)
        ],
        1,
    )
    proj_rows = shard // count
    proj_shard = lax.dynamic_slice_in_dim(w_proj[0], ci * proj_rows, proj_rows, 0)

    def fc_shard(duty):
        return jnp.concatenate(
            [
                lax.dynamic_slice_in_dim(
                    w_fc[0], owner * hidden_rows + ci * part + duty * half, half, 1
                )
                for owner in range(owners)
            ],
            1,
        )

    def out_shard(duty):
        return lax.dynamic_slice_in_dim(w_out[0], ci * part + duty * half, half, 0)

    qkv_shards = mine_other(qkv_shard, swap(qkv_shard, "section"))
    proj_shards = mine_other(proj_shard, swap(proj_shard, "section"))
    fc_shards = mine_other(fc_shard(xi), swap(fc_shard(1 - xi), "section"))
    out_shards = mine_other(out_shard(xi), swap(out_shard(1 - xi), "section"))

    def weights_of(layer):
        qkv_full = over_wt(qkv_shards[layer])
        proj_part = over_wt(proj_shards[layer], tiled=False)
        proj_full = jnp.swapaxes(by_owner(gathered(proj_part, "ctx"), "ctx"), 0, 1)
        proj_full = proj_full.reshape(width, width)
        fc_full = over_wt(fc_shards[layer])
        out_full = over_wt(out_shards[layer])
        return (
            qkv_full,
            proj_full,
            (fc_full, swap(fc_full, "section")),
            (out_full, swap(out_full, "section")),
        )

    weights = [weights_of(layer) for layer in range(2)]
    vectors = [vectors_of(layer) for layer in range(2)]
    kept = []
    state = entering
    for layer in range(2):
        state, kept_here = forward_layer(state, weights[layer], vectors[layer], plan, place, block)
        kept.append(kept_here)
    leaving = state

    def reduced(grads):
        g_w_qkv, g_w_proj, g_w_fc, g_w_out = grads
        fc_here = scatter_wt(g_w_fc[0] + swap(g_w_fc[1], "section"))
        out_here = scatter_wt(g_w_out[0] + swap(g_w_out[1], "section"))
        parts = g_w_proj.reshape(owners, count, proj_rows, width)
        parts = [lax.dynamic_index_in_dim(parts, ci ^ at, 1, keepdims=False) for at in range(count)]
        proj_here = scatter_wt(low(summed(parts, "ctx")), tiled=False)
        qkv_here = scatter_wt(g_w_qkv)
        return qkv_here, proj_here, fc_here, out_here

    def to_owner(late, early):
        there = swap(jnp.where(first, early, late), "section")
        return jnp.where(first, late, early), there

    weight_sums = [None, None]
    vector_grads = [None, None]
    for layer in (1, 0):
        coming, grads, vector_grads[layer] = backward_layer(
            coming, kept[layer], weights[layer], vectors[layer], plan, place, block
        )
        weight_sums[layer] = reduced(grads)

    def whole(value):
        return by_owner(gathered(value, "ctx"), "ctx")

    qkv_own, qkv_there = to_owner(weight_sums[0][0], weight_sums[1][0])
    proj_own, proj_there = to_owner(weight_sums[0][1], weight_sums[1][1])
    fc_own, fc_there = to_owner(weight_sums[0][2], weight_sums[1][2])
    out_own, out_there = to_owner(weight_sums[0][3], weight_sums[1][3])
    qkv_sum = wide(whole(low(wide(qkv_own) + wide(qkv_there)))).reshape(count, shard, 3, span)
    qkv_grad = jnp.concatenate([plan.joined(qkv_sum[:, :, at]) for at in range(3)], -1)
    proj_grad = wide(whole(low(wide(proj_own) + wide(proj_there)))).reshape(shard, width)
    fc_sum = jnp.where(first, jnp.stack([fc_own, fc_there]), jnp.stack([fc_there, fc_own]))
    fc_grad = wide(whole(fc_sum)).reshape(count, 2, shard, owners, half)
    fc_grad = fc_grad.transpose(2, 3, 0, 1, 4).reshape(shard, owners * hidden_rows)
    out_sum = jnp.where(
        first, jnp.concatenate([out_own, out_there]), jnp.concatenate([out_there, out_own])
    )
    out_grad = wide(whole(out_sum)).reshape(hidden_rows, width)

    def packed(grads):
        g_attn_gain, g_attn_shift, g_bias_qkv, g_proj_bias, g_mlp_gain, g_mlp_shift, g_fc, g_out = grads

        def placed(part):
            zeros = jnp.zeros((plan.padded,), jnp.float32)
            return lax.dynamic_update_slice_in_dim(zeros, part, ci * plan.step, 0)[:width]

        full = jnp.stack(
            [
                g_attn_gain,
                g_attn_shift,
                placed(g_bias_qkv[:span]),
                placed(g_bias_qkv[2 * span :]),
                g_proj_bias,
                g_mlp_gain,
                g_mlp_shift,
                g_out,
            ]
        )
        full = jnp.swapaxes(full.reshape(8, owners, shard), 0, 1).reshape(owners, 8 * shard)
        halves = [g.reshape(owners, half) for g in g_fc]
        halves = jnp.where(
            first, jnp.concatenate(halves, 1), jnp.concatenate(halves[::-1], 1)
        )
        zeros = jnp.zeros((owners, hidden_rows), jnp.float32)
        return jnp.concatenate(
            [full, lax.dynamic_update_slice_in_dim(zeros, halves, ci * part, 1)], 1
        )

    late, early = packed(vector_grads[0]), packed(vector_grads[1])
    total = jnp.where(first, late, early) + swap(jnp.where(first, early, late), "section")
    for bit in bits_of("ctx"):
        total = total + swap(total, "ctx", bit)
    pieces = {
        at: lax.dynamic_index_in_dim(total, plan.wi ^ at, 0, keepdims=False) for at in range(owners)
    }
    for bit in bits_of("wt"):
        for at in sorted(pieces, reverse=True):
            if at & bit:
                pieces[at ^ bit] = pieces[at ^ bit] + swap(pieces.pop(at), "wt", bit)
    total = pieces[0]
    vector_out = total[: 8 * shard].reshape(8, shard)
    fc_bias_out = total[8 * shard :]

    stays = jnp.where(first, coming, leaving)
    came = swap(jnp.where(first, leaving, coming), "section")
    result = jnp.where(first, jnp.stack([stays, came]), jnp.stack([came, stays]))
    result = result.reshape(1, 2, 1, rows, width)
    return (
        result,
        vector_out[0][None],
        vector_out[1][None],
        qkv_grad[None],
        vector_out[2][None],
        vector_out[3][None],
        proj_grad[None],
        vector_out[4][None],
        vector_out[5][None],
        vector_out[6][None],
        fc_grad[None],
        fc_bias_out[None],
        out_grad[None],
        vector_out[7][None],
    )


def solution(mesh):
    return jax.shard_map(
        body,
        mesh=mesh,
        in_specs=(
            P("section", None, "wt", "ctx", None),
            P(),
            P("section", "wt"),
            P("section", "wt"),
            P("section", "wt", None),
            P("section", "wt"),
            P("section", "wt"),
            P("section", "wt", None),
            P("section", "wt"),
            P("section", "wt"),
            P("section", "wt"),
            P("section", "wt", None),
            P("section", "wt"),
            P("section", "wt", None),
            P("section", "wt"),
        ),
        out_specs=(
            P("section", None, "wt", "ctx", None),
            P("section", "wt"),
            P("section", "wt"),
            P("section", "wt", None),
            P("section", "wt"),
            P("section", "wt"),
            P("section", "wt", None),
            P("section", "wt"),
            P("section", "wt"),
            P("section", "wt"),
            P("section", "wt", None),
            P("section", "wt"),
            P("section", "wt", None),
            P("section", "wt"),
        ),
        check_vma=False,
    )
```

```python
import functools
import math

import jax
import jax.numpy as jnp
from jax import lax
from jax.experimental import pallas as pl
from jax.experimental.pallas import tpu as pltpu
from jax.sharding import PartitionSpec as P

SECTION, CTX, WT = "section", "ctx", "wt"
QKV, PROJ, FC, OUT = range(4)
OWN, NORM, SCORES, MIXED, GATHERED, ACTIVE, RESULT = range(7)
START, HIDDEN, SECOND, SUM, HEADS, BACK, THERE, FIRST, END = range(9)
FULL, MOVED, SEND, CAME, REDUCE, DONE, HOP, OWNED, TOKEN = range(9)

HEAD_DIM = 64
NEG = -1000000000.0
LANES = 128


def nt_dot(left, right):
    return lax.dot_general(left, right, (((1,), (1,)), ((), ())), preferred_element_type=jnp.float32)


def nn_dot(left, right):
    return jnp.dot(left, right, preferred_element_type=jnp.float32)


def causal_scores(keys, query, tile):
    scores = nt_dot(keys, query)
    edge = scores.shape[0] - tile
    key_at = lax.broadcasted_iota(jnp.int32, (tile, tile), 0)
    query_at = lax.broadcasted_iota(jnp.int32, (tile, tile), 1)
    last = jnp.where(key_at <= query_at, scores[edge:], NEG)
    return jnp.concatenate([scores[:edge], last], 0) if edge else last


def attend_kernel(block, tile, heads, place, qkv, out, log_total, query, keyed, valued, mixed):
    length, three = qkv.shape
    span = three // 3
    lane = lax.broadcasted_iota(jnp.int32, (tile, LANES), 1)

    def pair(index, carry):
        start = pl.multiple_of(index * LANES, LANES)
        for at in range(length // block):
            rows = pl.ds(pl.multiple_of(place[at] * block, block), block)
            here = pl.ds(at * block, block)
            query[here, :] = qkv[rows, pl.ds(start, LANES)] * (HEAD_DIM ** (-0.5))
            keyed[here, :] = qkv[rows, pl.ds(span + start, LANES)]
            valued[:, here] = qkv[rows, pl.ds(2 * span + start, LANES)].T

        for half in range(2):

            @pl.when(2 * index + half < heads)
            def _():
                mine = (lane < HEAD_DIM) if half == 0 else (lane >= HEAD_DIM)
                features = slice(half * HEAD_DIM, (half + 1) * HEAD_DIM)
                for at in range(length // tile):
                    seen = (at + 1) * tile
                    cols = slice(at * tile, seen)
                    part = jnp.where(mine, query[cols, :], 0)
                    scores = causal_scores(keyed[:seen, :], part, tile)
                    highest = jnp.max(scores, 0, keepdims=True)
                    exponent = jnp.exp(scores - highest)
                    total = jnp.sum(exponent, 0, keepdims=True)
                    result = nn_dot(valued[features, :seen], exponent.astype(jnp.bfloat16))
                    mixed[features, cols] = result * (1.0 / total)
                    log_total[pl.ds(2 * index + half, 1), cols] = highest + jnp.log(total)

        for at in range(length // block):
            rows = pl.ds(pl.multiple_of(place[at] * block, block), block)
            out[rows, pl.ds(start, LANES)] = mixed[:, at * block : (at + 1) * block].T.astype(out.dtype)
        return carry

    mixed[...] = jnp.zeros_like(mixed)
    lax.fori_loop(0, span // LANES, pair, 0)


def attend(place, qkv, heads, block):
    length, three = qkv.shape
    span = three // 3
    tile = min(256, length)
    rows = -(-span // HEAD_DIM // 8) * 8
    vmem = pl.BlockSpec(memory_space=pltpu.VMEM)
    return pl.pallas_call(
        functools.partial(attend_kernel, block, tile, heads),
        out_shape=(
            jax.ShapeDtypeStruct((length, span), jnp.bfloat16),
            jax.ShapeDtypeStruct((rows, length), jnp.float32),
        ),
        in_specs=[pl.BlockSpec(memory_space=pltpu.SMEM), vmem],
        out_specs=(vmem, vmem),
        scratch_shapes=[
            pltpu.VMEM((length, LANES), jnp.bfloat16),
            pltpu.VMEM((length, LANES), jnp.bfloat16),
            pltpu.VMEM((LANES, length), jnp.bfloat16),
            pltpu.VMEM((LANES, length), jnp.float32),
        ],
        compiler_params=pltpu.CompilerParams(vmem_limit_bytes=40 * 1024 * 1024),
        cost_estimate=pl.CostEstimate(
            flops=0, bytes_accessed=0, transcendentals=0
        ),
    )(place, qkv)


def attend_back_kernel(
    block, tile, heads, place, qkv, grad_mixed, log_total, out,
    query, keyed, keyed_t, valued, grad, grad_query, grad_key, grad_value,
):
    length, three = qkv.shape
    span = three // 3
    scale = HEAD_DIM ** (-0.5)
    lane = lax.broadcasted_iota(jnp.int32, (tile, LANES), 1)

    def pair(index, carry):
        start = pl.multiple_of(index * LANES, LANES)
        for at in range(length // block):
            rows = pl.ds(pl.multiple_of(place[at] * block, block), block)
            here = pl.ds(at * block, block)
            query[here, :] = qkv[rows, pl.ds(start, LANES)] * scale
            key_part = qkv[rows, pl.ds(span + start, LANES)]
            keyed[here, :] = key_part
            keyed_t[:, here] = key_part.T
            valued[here, :] = qkv[rows, pl.ds(2 * span + start, LANES)]
            grad[here, :] = grad_mixed[rows, pl.ds(start, LANES)]
        grad_query[...] = jnp.zeros_like(grad_query)
        grad_key[...] = jnp.zeros_like(grad_key)
        grad_value[...] = jnp.zeros_like(grad_value)

        for half in range(2):

            @pl.when(2 * index + half < heads)
            def _():
                mine = (lane < HEAD_DIM) if half == 0 else (lane >= HEAD_DIM)
                features = slice(half * HEAD_DIM, (half + 1) * HEAD_DIM)
                for at in range(length // tile):
                    seen = (at + 1) * tile
                    cols = slice(at * tile, seen)
                    part = jnp.where(mine, query[cols, :], 0)
                    grad_part = jnp.where(mine, grad[cols, :], 0)
                    scores = causal_scores(keyed[:seen, :], part, tile)
                    chance = jnp.exp(scores - log_total[pl.ds(2 * index + half, 1), cols])
                    grad_chance = nt_dot(valued[:seen, :], grad_part)
                    inner = jnp.sum(chance * grad_chance, 0, keepdims=True)
                    grad_scores = (chance * (grad_chance - inner)).astype(jnp.bfloat16)
                    grad_value[:seen, :] += nn_dot(chance.astype(jnp.bfloat16), grad_part)
                    grad_key[:seen, :] += nn_dot(grad_scores, part)
                    grad_query[features, cols] = nn_dot(keyed_t[features, :seen], grad_scores) * scale

        for at in range(length // block):
            rows = pl.ds(pl.multiple_of(place[at] * block, block), block)
            here = slice(at * block, (at + 1) * block)
            out[rows, pl.ds(start, LANES)] = grad_query[:, here].T.astype(out.dtype)
            out[rows, pl.ds(span + start, LANES)] = grad_key[here, :].astype(out.dtype)
            out[rows, pl.ds(2 * span + start, LANES)] = grad_value[here, :].astype(out.dtype)
        return carry

    lax.fori_loop(0, span // LANES, pair, 0)


def attend_back(place, qkv, grad_mixed, log_total, heads, block):
    length, three = qkv.shape
    span = three // 3
    tile = min(256, length)
    vmem = pl.BlockSpec(memory_space=pltpu.VMEM)
    return pl.pallas_call(
        functools.partial(attend_back_kernel, block, tile, heads),
        out_shape=jax.ShapeDtypeStruct((length, three), jnp.bfloat16),
        in_specs=[pl.BlockSpec(memory_space=pltpu.SMEM), vmem, vmem, vmem],
        out_specs=vmem,
        scratch_shapes=[
            pltpu.VMEM((length, LANES), jnp.bfloat16),
            pltpu.VMEM((length, LANES), jnp.bfloat16),
            pltpu.VMEM((LANES, length), jnp.bfloat16),
            pltpu.VMEM((length, LANES), jnp.bfloat16),
            pltpu.VMEM((length, LANES), jnp.bfloat16),
            pltpu.VMEM((LANES, length), jnp.float32),
            pltpu.VMEM((length, LANES), jnp.float32),
            pltpu.VMEM((length, LANES), jnp.float32),
        ],
        compiler_params=pltpu.CompilerParams(vmem_limit_bytes=48 * 1024 * 1024),
        cost_estimate=pl.CostEstimate(
            flops=0, bytes_accessed=0, transcendentals=0
        ),
    )(place, qkv, grad_mixed, log_total)


EPS = 1e-05
GELU_A = math.sqrt(2.0 / math.pi)
GELU_B = 0.044715


def flip(axis, bit):
    return [(at, at ^ bit) for at in range(lax.axis_size(axis))]


def swap(value, axis, bit=1):
    return lax.ppermute(value, axis, flip(axis, bit))


def bits_of(axis):
    bits, bit = [], 1
    while bit < lax.axis_size(axis):
        bits.append(bit)
        bit *= 2
    return bits


def gathered(value, axis):
    pieces = {0: value}
    for bit in reversed(bits_of(axis)):
        for at in list(pieces):
            pieces[at | bit] = swap(pieces[at], axis, bit)
    return [pieces[at] for at in range(lax.axis_size(axis))]


def gathered_whole(value, axis):
    pieces = {0: value}
    for bit in reversed(bits_of(axis)):
        held = list(pieces)
        for at, came in zip(held, together([pieces[at] for at in held], axis, bit)):
            pieces[at | bit] = came
    return [pieces[at] for at in range(lax.axis_size(axis))]


def together(pieces, axis, bit):
    if len(pieces) == 1:
        return [swap(pieces[0], axis, bit)]
    came = swap(jnp.concatenate(pieces), axis, bit)
    rows = pieces[0].shape[0]
    return [came[at * rows : (at + 1) * rows] for at in range(len(pieces))]


def summed(pieces, axis, bits=None):
    pieces = dict(pieces) if isinstance(pieces, dict) else dict(enumerate(pieces))
    for bit in bits_of(axis) if bits is None else bits:
        for at in sorted(pieces, reverse=True):
            if at & bit:
                came = swap(pieces.pop(at).astype(jnp.bfloat16), axis, bit)
                pieces[at ^ bit] = pieces[at ^ bit].astype(jnp.float32) + came.astype(jnp.float32)
    return pieces[0] if len(pieces) == 1 else pieces


def exchanged(pieces, axis):
    return [swap(piece, axis, at) if at else piece for at, piece in enumerate(pieces)]


def at_once(go, step, operands, aside=None):
    aside = aside or []
    counts = [len(inputs) for unused, inputs in aside]

    def both(operands, inputs):
        results, at = [], 0
        for (work, unused), count in zip(aside, counts):
            results.append(work(*inputs[at : at + count]))
            at += count
        return step(*operands), results

    inputs = [value for unused, values in aside for value in values]
    shapes = jax.eval_shape(both, operands, inputs)

    def nothing(*unused):
        return jax.tree.map(lambda shape: jnp.zeros(shape.shape, shape.dtype), shapes)

    return lax.cond(go, both, nothing, operands, inputs)


def by_owner(pieces, axis):
    here = lax.axis_index(axis)
    whole = jnp.zeros((len(pieces),) + pieces[0].shape, pieces[0].dtype)
    for at, piece in enumerate(pieces):
        whole = lax.dynamic_update_index_in_dim(whole, piece, here ^ at, 0)
    return whole


def after(value, *marks):
    return lax.optimization_barrier(marks + (value,))[-1]


def tied(*values):
    return lax.optimization_barrier(values)


def over_wt(value, tiled=True):
    return lax.all_gather(value, WT, axis=0, tiled=tiled)


def scatter_wt(value, tiled=True):
    return lax.psum_scatter(value, WT, scatter_dimension=0, tiled=tiled)


def dot(left, right):
    return jnp.dot(left, right, preferred_element_type=jnp.float32)


def dot_nt(left, right):
    return lax.dot_general(left, right, (((1,), (1,)), ((), ())), preferred_element_type=jnp.float32)


def dot_tn(left, right):
    return lax.dot_general(left, right, (((0,), (0,)), ((), ())), preferred_element_type=jnp.float32)


def low(value):
    return value.astype(jnp.bfloat16)


def wide(value):
    return value.astype(jnp.float32)


def normed(values):
    center = values - jnp.mean(values, -1, keepdims=True)
    rate = lax.rsqrt(jnp.mean(center * center, -1, keepdims=True) + EPS)
    return center * rate, rate


def norm_back(grad, gain, values):
    unit, rate = normed(values)
    inner = grad * gain
    back = (
        inner
        - jnp.mean(inner, -1, keepdims=True)
        - unit * jnp.mean(inner * unit, -1, keepdims=True)
    ) * rate
    return back, jnp.sum(grad * unit, 0), jnp.sum(grad, 0)


def gelu(value):
    return 0.5 * value * (1.0 + jnp.tanh(GELU_A * (value + GELU_B * value * value * value)))


def gelu_slope(value):
    square = value * value
    bend = jnp.tanh(GELU_A * (value + GELU_B * value * square))
    return 0.5 * (1.0 + bend) + 0.5 * value * (1.0 - bend * bend) * (
        GELU_A * (1.0 + 3.0 * GELU_B * square)
    )


def joined_kernel(count, segments, at, *refs):
    out, pieces = refs[-1], refs[:-1]
    kinds = len(pieces) // count
    picked = {}
    for kind, owner, source, target, columns in segments:
        if (kind, owner) not in picked:
            value = pieces[kind * count][...].astype(jnp.float32)
            for step in range(1, count):
                other = pieces[kind * count + step][...].astype(jnp.float32)
                value = jnp.where((at[0] ^ owner) == step, other, value)
            picked[kind, owner] = value
        out[:, target : target + columns] = picked[kind, owner][:, source : source + columns]
    assert kinds * count == len(pieces)


def joined_columns(pieces, segments, ci, columns):
    flat = [piece for kind in pieces for piece in kind]
    rows = flat[0].shape[0]
    tile = 80 if rows % 80 == 0 else rows
    return pl.pallas_call(
        functools.partial(joined_kernel, len(pieces[0]), segments),
        out_shape=jax.ShapeDtypeStruct((rows, columns), jnp.float32),
        grid=(rows // tile,),
        in_specs=[pl.BlockSpec(memory_space=pltpu.SMEM)]
        + [pl.BlockSpec((tile, piece.shape[1]), lambda at: (at, 0)) for piece in flat],
        out_specs=pl.BlockSpec((tile, columns), lambda at: (at, 0)),
        compiler_params=pltpu.CompilerParams(vmem_limit_bytes=48 * 1024 * 1024),
        cost_estimate=pl.CostEstimate(
            flops=0, bytes_accessed=6 * rows * columns, transcendentals=0
        ),
    )(ci.reshape(1), *flat)


class Plan:
    def __init__(self, width, hidden_rows, go):
        self.go = go
        self.count = lax.axis_size(CTX)
        self.ci = lax.axis_index(CTX)
        self.first = lax.axis_index(SECTION) == 0
        self.xi = lax.axis_index(SECTION)
        self.wi = lax.axis_index(WT)
        self.width = width
        heads = width // HEAD_DIM
        stride = heads // self.count
        self.heads = heads - stride * (self.count - 1)
        self.step = stride * HEAD_DIM
        self.span = (self.heads + self.heads % 2) * HEAD_DIM
        self.padded = self.step * (self.count - 1) + self.span
        self.owned = jnp.where(self.ci == self.count - 1, self.heads, stride) * HEAD_DIM
        self.part = hidden_rows // self.count
        self.half = self.part // 2
        self.shard = width // lax.axis_size(WT)
        self.proj_rows = -(-self.shard // self.count // 16) * 16

    def proj_start(self, index):
        return jnp.minimum(index * self.proj_rows, self.shard - self.proj_rows)

    def gathered(self, value):
        def step(value):
            return gathered(value, CTX)[1:]

        return [value] + at_once(self.go, step, [value])[0]

    def exchanged(self, pieces, aside=None):
        def step(*pieces):
            return [swap(piece, CTX, at + 1) for at, piece in enumerate(pieces)]

        came, extra = at_once(self.go, step, pieces[1:], aside)
        return pieces[:1] + came, extra

    def summed(self, value, aside=None):
        def step(value):
            return wide(summed(cut(value, self.count), CTX))

        return at_once(self.go, step, [value], aside)

    def proj_parts(self, left, right):
        parts = grad_dot(left, right).reshape(-1, self.shard, self.width)
        return [
            lax.dynamic_slice_in_dim(parts, self.proj_start(self.ci ^ at), self.proj_rows, 1)
            for at in range(self.count)
        ]

    def padded_out(self, array):
        return jnp.pad(array, [(0, 0)] * (array.ndim - 1) + [(0, self.padded - array.shape[-1])])

    def window(self, padded, index):
        return lax.dynamic_slice_in_dim(padded, index * self.step, self.span, padded.ndim - 1)

    def joined(self, ordered):
        last = self.width - self.step * (self.count - 1)
        parts = [ordered[at, ..., : self.step] for at in range(self.count - 1)]
        return jnp.concatenate(parts + [ordered[self.count - 1, ..., :last]], -1)


def joined_rows_kernel(at, *refs):
    out, pieces = refs[-1], refs[:-1]
    step = pl.program_id(0)
    for index, piece in enumerate(pieces):

        @pl.when(step == index)
        def _():
            out[...] = piece[...].astype(jnp.float32)


def joined_rows(pieces, ci):
    rows, columns = pieces[0].shape
    count = len(pieces)
    if rows % 8:
        return wide(by_owner(pieces, CTX)).reshape(count * rows, columns)
    return pl.pallas_call(
        joined_rows_kernel,
        out_shape=jax.ShapeDtypeStruct((count * rows, columns), jnp.float32),
        grid_spec=pltpu.PrefetchScalarGridSpec(
            num_scalar_prefetch=1,
            grid=(count,),
            in_specs=[pl.BlockSpec((rows, columns), lambda step, at: (0, 0))] * count,
            out_specs=pl.BlockSpec((rows, columns), lambda step, at: (at[0] ^ step, 0)),
        ),
        compiler_params=pltpu.CompilerParams(vmem_limit_bytes=48 * 1024 * 1024),
        cost_estimate=pl.CostEstimate(
            flops=0, bytes_accessed=6 * count * rows * columns, transcendentals=0
        ),
    )(ci.reshape(1), *pieces)


def placed_kernel(owners, start, *refs):
    out, pieces = refs[-1], refs[:-1]
    rows = pieces[0].shape[0] // owners
    shard = out.shape[0] // owners
    for at, piece in enumerate(pieces):
        for owner in range(owners):
            here = pl.ds(pl.multiple_of(owner * shard + start[at], 16), rows)
            out[here, :] = piece[owner * rows : (owner + 1) * rows, :].astype(out.dtype)


def placed_rows(pieces, starts, owners, shard, dtype):
    columns = pieces[0].shape[1]
    vmem = pl.BlockSpec(memory_space=pltpu.VMEM)
    return pl.pallas_call(
        functools.partial(placed_kernel, owners),
        out_shape=jax.ShapeDtypeStruct((owners * shard, columns), dtype),
        in_specs=[pl.BlockSpec(memory_space=pltpu.SMEM)] + [vmem] * len(pieces),
        out_specs=vmem,
        compiler_params=pltpu.CompilerParams(vmem_limit_bytes=48 * 1024 * 1024),
        cost_estimate=pl.CostEstimate(
            flops=0, bytes_accessed=4 * owners * shard * columns, transcendentals=0
        ),
    )(jnp.stack(starts), *pieces)


def cut(value, count):
    rows = value.shape[0] // count
    return [value[at * rows : (at + 1) * rows] for at in range(count)]


def forward_layer(entering, weight, vectors, plan, place, block, pin):
    attn_gain, attn_shift, bias_qkv, proj_bias, mlp_gain, mlp_shift, fc_bias, out_bias = vectors
    stream = wide(entering)
    first_norm = pin(OWN, low(normed(stream)[0] * attn_gain + attn_shift))
    first_norm = jnp.concatenate(pin(NORM, plan.gathered(first_norm)))
    qkv = pin(SCORES, low(dot(first_norm, weight(QKV)) + bias_qkv))
    mixed, log_total = attend(place, qkv, plan.heads, block)
    mixed = pin(MIXED, mixed)
    mixed_all = plan.joined(by_owner(plan.exchanged(cut(mixed, plan.count))[0], CTX))
    middle = (dot(mixed_all, weight(PROJ)) + proj_bias) + stream
    second_norm = low(normed(middle)[0] * mlp_gain + mlp_shift)
    second_norm = jnp.concatenate(pin(GATHERED, plan.gathered(second_norm)))
    hidden = [dot(second_norm, part) + bias for part, bias in zip(weight(FC), fc_bias)]
    active = pin(ACTIVE, [low(gelu(part)) for part in hidden])

    def final(first_marks=(), last_marks=()):
        parts = after(active, *first_marks)
        w_out = weight(OUT)
        result = pin(RESULT, low(dot(parts[0], w_out[0]) + dot(parts[1], w_out[1])))
        return low((plan.summed(after(result, *last_marks))[0] + out_bias) + middle)

    kept = (stream, first_norm, qkv, log_total, mixed_all, middle, second_norm, hidden, active)
    return final, kept


def grad_dot(left, right):
    return low(dot_tn(left, right))


def grad_dot_all(left, *right):
    return low(dot_tn(left, jnp.concatenate(right)))


def backward_layer(coming, coming_all, kept, weight, vectors, plan, place, block, pin, aside):
    attn_gain, attn_shift, bias_qkv, proj_bias, mlp_gain, mlp_shift, fc_bias, out_bias = vectors
    stream, first_norm, qkv, log_total, mixed_all, middle, second_norm, hidden, active = kept
    grads, sums = {}, {}
    w_fc, w_out = weight(FC), weight(OUT)
    grads[OUT] = [(grad_dot_all, [part] + coming_all) for part in active]
    coming_all = pin(START, coming_all, grads)
    grads[OUT] = [(grad_dot_all, [part] + coming_all) for part in active]
    coming_whole = jnp.concatenate(coming_all)
    grad_hidden = [
        low(dot_nt(coming_whole, part) * gelu_slope(at)) for part, at in zip(w_out, hidden)
    ]
    grads[FC] = [(grad_dot, [second_norm, part]) for part in grad_hidden]
    grad_hidden = pin(HIDDEN, grad_hidden, grads)
    grads[FC] = [(grad_dot, [second_norm, part]) for part in grad_hidden]
    grad_second = low(dot_nt(grad_hidden[0], w_fc[0]) + dot_nt(grad_hidden[1], w_fc[1]))
    grad_second = pin(SECOND, grad_second, grads)
    grad_norm = aside(SUM, lambda extra: plan.summed(grad_second, extra), grads)
    grad_norm = pin(SUM, grad_norm, grads)
    back, sums["mlp_gain"], sums["mlp_shift"] = norm_back(grad_norm, mlp_gain, middle)
    grad_final = wide(coming)
    grad_middle = back + grad_final
    branch = low(grad_middle)
    grad_mixed = plan.padded_out(low(dot_nt(branch, weight(PROJ))))
    pieces = [plan.window(grad_mixed, plan.ci ^ at) for at in range(plan.count)]
    grads[PROJ] = [(plan.proj_parts, [mixed_all, branch])]
    grad_heads = aside(HEADS, lambda extra: plan.exchanged(pieces, extra), grads)
    grad_heads = jnp.concatenate(grad_heads)
    column = lax.broadcasted_iota(jnp.int32, grad_heads.shape, 1)
    grad_heads = pin(HEADS, jnp.where(column < plan.owned, grad_heads, 0), grads)
    grad_qkv = attend_back(place, qkv, grad_heads, log_total, plan.heads, block)
    grad_qkv = pin(BACK, grad_qkv, grads)
    grads[QKV] = [(grad_dot, [first_norm, grad_qkv])]
    grad_qkv = pin(THERE, grad_qkv, grads)
    grad_first = pin(FIRST, low(dot_nt(grad_qkv, weight(QKV))), grads)
    grad_norm = aside(END, lambda extra: plan.summed(grad_first, extra), grads)
    grad_norm = pin(END, grad_norm, grads)
    back, sums["attn_gain"], sums["attn_shift"] = norm_back(grad_norm, attn_gain, stream)
    leaving = low(back + grad_middle)
    sums["fc"] = [jnp.sum(wide(part), 0) for part in grad_hidden]
    sums["out"] = jnp.sum(grad_final, 0)
    sums["proj"] = jnp.sum(wide(branch), 0)
    sums["qkv"] = jnp.sum(wide(grad_qkv), 0)
    return leaving, sums


def body(
    feed,
    block_order,
    attn_gain,
    attn_shift,
    w_qkv,
    query_bias,
    value_bias,
    w_proj,
    proj_bias,
    mlp_gain,
    mlp_shift,
    w_fc,
    fc_bias,
    w_out,
    out_bias,
):
    width = w_proj.shape[2]
    shard = w_proj.shape[1]
    hidden_rows = w_out.shape[1]
    plan = Plan(width, hidden_rows, block_order[0] >= 0)
    count, owners = plan.count, lax.axis_size(WT)
    first, xi, ci = plan.first, plan.xi, plan.ci
    part, half, span = plan.part, plan.half, plan.span
    rows = feed.shape[3]
    block = rows // 2

    def mine_other(mine, other):
        return (jnp.where(first, mine, other), jnp.where(first, other, mine))

    slots = jnp.arange(2 * count, dtype=jnp.int32)
    held = 2 * (ci ^ (slots // 2)) + slots % 2
    table = (held[:, None] == slots[None, :]).astype(jnp.int32)
    blocks_held = jnp.sum(table * block_order[None, :], 1)
    found = (blocks_held[None, :] == slots[:, None]).astype(jnp.int32)
    place = jnp.sum(found * slots[None, :], 1)

    fc_part = lax.dynamic_slice_in_dim(fc_bias[0], ci * part, part, 0)
    names = (attn_gain, attn_shift, query_bias, value_bias, proj_bias, mlp_gain, mlp_shift, out_bias)
    small = jnp.concatenate([vector[0] for vector in names] + [fc_part])
    local = feed[0, :, 0]
    feed_own = lax.dynamic_index_in_dim(local, xi, 0, keepdims=False)
    feed_gone = lax.dynamic_index_in_dim(local, 1 - xi, 0, keepdims=False)

    def fc_shard(duty):
        return jnp.concatenate(
            [
                lax.dynamic_slice_in_dim(
                    w_fc[0], owner * hidden_rows + ci * part + duty * half, half, 1
                )
                for owner in range(owners)
            ],
            1,
        )

    def out_shard(duty):
        return lax.dynamic_slice_in_dim(w_out[0], ci * part + duty * half, half, 0)

    qkv_shard = jnp.concatenate(
        [
            plan.window(plan.padded_out(w_qkv[0][:, at * width : (at + 1) * width]), ci)
            for at in range(3)
        ],
        1,
    )
    proj_shard = lax.dynamic_slice_in_dim(w_proj[0], plan.proj_start(ci), plan.proj_rows, 0)

    def qkv_half(duty):
        return lax.dynamic_slice_in_dim(qkv_shard, duty * (shard // 2), shard // 2, 0)

    whole_here = {(OUT, 1)}
    own_shards = {QKV: qkv_half(xi), PROJ: proj_shard, FC: fc_shard(xi), OUT: out_shard(xi)}
    gone = {QKV: qkv_half(1 - xi), PROJ: proj_shard, FC: fc_shard(1 - xi), OUT: out_shard(1 - xi)}
    came = {QKV: swap(gone[QKV], SECTION)}
    started = [came[QKV]]
    feed_gone = after(feed_gone, gone[QKV])
    feed_came = swap(feed_gone, SECTION)
    small_came = swap(after(small, feed_gone), SECTION)
    started += [feed_came, small_came]
    before = feed_gone
    for name in (PROJ, FC, OUT):
        before = after(gone[name], before)
        came[name] = swap(before, SECTION)
        started.append(came[name])
    shards = {name: mine_other(own_shards[name], came[name]) for name in (QKV, PROJ)}
    last_gone = after(own_shards[OUT], before)
    last_came = swap(last_gone, SECTION)

    entering, coming = mine_other(feed_own, feed_came)
    small = jnp.stack(mine_other(small, small_came))
    small = wide(by_owner(gathered(small, WT), WT))

    def vectors_of(layer):
        full = jnp.swapaxes(small[:, layer, : 8 * shard].reshape(owners, 8, shard), 0, 1)
        full = full.reshape(8, owners * shard)
        hidden = small[:, layer, 8 * shard :]
        halves = [
            lax.dynamic_slice_in_dim(hidden, duty * half, half, 1).reshape(-1) for duty in (xi, 1 - xi)
        ]
        query = plan.window(plan.padded_out(full[2]), ci)
        value = plan.window(plan.padded_out(full[3]), ci)
        bias_qkv = jnp.concatenate([query, jnp.zeros_like(query), value])
        return (full[0], full[1], bias_qkv, full[4], full[5], full[6], halves, full[7])

    vectors = [vectors_of(layer) for layer in range(2)]
    full, operands = {}, []
    tiny = small_came[:128]

    def gather_over_wt(keys, *marks):
        for key in keys:
            name, layer = key
            piece = after(shards[name][layer], *operands[-1:], *marks)
            operands.append(piece)
            full[key] = over_wt(piece)
            started.append(full[key])

    gather_over_wt([(QKV, 0)])
    gather_over_wt([(PROJ, 0)], feed_came, small_came)

    made, moved = {}, {}

    def move(key):
        if key not in moved:
            value = full[key]
            if key[0] == PROJ:
                moved[key] = gathered(value, CTX)
            elif key in whole_here:
                moved[key] = None
            else:
                moved[key] = swap(value, SECTION)
            started.append(moved[key])
        return moved[key]

    def weight(layer, name):
        key = (name, layer)
        if key in made:
            return made[key]
        other, value = move(key), full[key]
        if name == QKV:
            halves = [part.reshape(owners, shard // 2, 3 * span) for part in mine_other(value, other)]
            result = jnp.stack(halves, 1).reshape(width, 3 * span)
        elif name == PROJ:
            starts = [plan.proj_start(ci ^ at) for at in range(count)]
            result = placed_rows(other, starts, owners, shard, jnp.bfloat16)
        elif key in whole_here:
            result = tuple(value[:, at].reshape(-1, value.shape[-1]) for at in range(2))
        else:
            result = (value, other)
        made[key] = result
        return result

    front = {
        (0, OWN): ((FULL, QKV, 0),),
        (0, NORM): ((FULL, PROJ, 0),),
        (0, MIXED): ((MOVED, PROJ, 0), (FULL, FC, 0)),
        (0, GATHERED): ((MOVED, FC, 0), (FULL, OUT, 0)),
        (0, ACTIVE): ((FULL, PROJ, 1),),
        (0, RESULT): ((MOVED, PROJ, 1), (FULL, QKV, 1)),
        (1, NORM): ((MOVED, QKV, 1), (FULL, FC, 1)),
        (1, GATHERED): ((MOVED, FC, 1),),
    }

    def forward_pin(layer):
        def pin(point, value):
            if (layer, point) == (0, OWN):
                for name in (FC, OUT):
                    shards[name] = mine_other(own_shards[name], after(came[name], value))
                keys = [(FC, 0), (OUT, 0), (PROJ, 1), (QKV, 1), (FC, 1)]
                gather_over_wt(keys, value)
            if (layer, point) == (0, MIXED):
                last, value = tied(last_came, value)
                shards[OUT, 1] = jnp.stack([shards[OUT][1], mine_other(gone[OUT], last)[1]])
            if (layer, point) == (0, ACTIVE):
                piece, value = tied(shards[OUT, 1], value)
                full[OUT, 1] = over_wt(after(piece, operands[-1]), tiled=False)
                started.append(full[OUT, 1])
            for kind, *key in front.get((layer, point), ()):
                key = tuple(key)
                if kind == FULL:
                    full[key], value = tied(full[key], value)
                    move(key)
                else:
                    moved[key], value = tied(moved[key], value)
            return value

        return pin

    kept = []
    state = entering
    for layer in range(2):
        state, kept_here = forward_layer(
            state,
            functools.partial(weight, layer),
            vectors[layer],
            plan,
            place,
            block,
            forward_pin(layer),
        )
        kept.append(kept_here)
        if layer == 0:
            state = state()

    whole_sums = {(OUT, 1)}
    dots, sent, ready, sums, hops, order = {}, {}, {}, {}, {}, []

    def grad_of(key, at, grads):
        if (key, at) not in dots:
            work, inputs = grads[key[0]][at]
            dots[key, at] = work(*inputs)
        return dots[key, at]

    def prepared(key, grads):
        if key[0] == QKV:
            parts = grad_of(key, 0, grads).reshape(owners, 2, shard // 2, 3 * span)
            mine, away = (
                lax.dynamic_index_in_dim(parts, at, 1, keepdims=False).reshape(-1, 3 * span)
                for at in (xi, 1 - xi)
            )
            dots[key, QKV] = mine
            return away
        if key[0] == PROJ:
            return grad_of(key, 0, grads)
        if key in whole_sums:
            halves = [grad_of(key, at, grads).reshape(owners, half, width) for at in range(2)]
            return jnp.stack(halves, 1).reshape(-1, width)
        return grad_of(key, 1, grads)

    def core(*parts):
        return summed(parts, CTX, bits_of(CTX)[:-1])

    def start(key, away):
        if key[0] == PROJ:
            sent[key] = summed(away, CTX, bits_of(CTX)[-1:])
        elif key in whole_sums:
            sent[key] = away
        else:
            sent[key] = swap(away, SECTION)
        started.append(sent[key])

    def add(key, grads):
        came = sent[key]
        if key[0] == PROJ:
            return low(came).reshape(-1, width)
        if key in whole_sums:
            return came
        mine = dots[key, QKV] if key[0] == QKV else grad_of(key, 0, grads)
        return low(wide(came) + wide(mine))

    def hop(key):
        if key not in hops:
            hops[key] = lax.ppermute(sums[key], SECTION, [(1 - key[1], key[1])])
            started.append(hops[key])
        return hops[key]

    def both_halves(key):
        value, came = sums[key], hop(key)
        rows = value.shape[0]
        if key in whole_sums:
            rows = rows // 2
            own = low(wide(value[:rows]) + wide(came[rows:]))
            came = low(wide(value[rows:]) + wide(came[:rows]))
            value = own
        return (value, came) if key[1] == 0 else (came, value)

    def ordered(name):
        late, early = both_halves((name, 0)), both_halves((name, 1))
        return tuple(jnp.where(first, a, b) for a, b in zip(late, early))

    owned = {}
    back = {
        (1, START): ((SEND, OUT, 1), (CAME, OUT, 1), (REDUCE, OUT, 1)),
        (1, HIDDEN): ((SEND, FC, 1),),
        (1, HEADS): ((CAME, FC, 1), (SEND, PROJ, 1), (TOKEN,)),
        (1, BACK): ((DONE, OUT, 1), (REDUCE, FC, 1)),
        (1, FIRST): ((CAME, PROJ, 1),),
        (1, END): ((HOP, OUT, 1), (REDUCE, PROJ, 1), (SEND, QKV, 1), (TOKEN,)),
        (0, START): ((DONE, FC, 1), (SEND, OUT, 0)),
        (0, HIDDEN): ((CAME, QKV, 1),),
        (0, SECOND): ((REDUCE, QKV, 1),),
        (0, SUM): ((CAME, OUT, 0), (SEND, FC, 0), (TOKEN,), (DONE, PROJ, 1)),
        (0, HEADS): ((REDUCE, OUT, 0), (SEND, PROJ, 0), (TOKEN,)),
        (0, BACK): ((DONE, QKV, 1), (DONE, OUT, 0), (CAME, FC, 0), (REDUCE, FC, 0)),
        (0, THERE): ((SEND, QKV, 0), (TOKEN,), (HOP, OUT, 0)),
        (0, FIRST): ((CAME, PROJ, 0), (OWNED, OUT, 0)),
    }
    beside = {
        (1, HEADS): ((PROJ, 0),),
        (1, END): ((QKV, 0),),
        (0, SUM): ((OUT, 0),),
        (0, HEADS): ((PROJ, 0),),
    }

    def backward_pin(layer):
        def pin(point, value, grads):
            for kind, *key in back.get((layer, point), ()):
                key = tuple(key)
                if kind == SEND:
                    away = prepared(key, grads)
                    if key[0] == PROJ:
                        away = at_once(plan.go, core, away)[0]
                    away, value = tied(away, value)
                    start(key, away)
                elif kind == CAME:
                    sent[key], value = tied(sent[key], value)
                    ready[key] = add(key, grads if key[1] == layer else all_grads[key[1]])
                elif kind == TOKEN:
                    token, value = tied(tiny, value)
                    token, value = tied(swap(token, CTX), value)
                    started.append(token)
                elif kind == OWNED:
                    whole, value = tied(jnp.concatenate(ordered(key[0])), value)
                    owned[key[0]] = gathered_whole(whole, CTX)
                elif kind == HOP:
                    hops[key], value = tied(hop(key), value)
                elif kind == DONE:
                    sums[key], value = tied(sums[key], value)
                elif kind == REDUCE:
                    if order:
                        ready[key] = after(ready[key], ready[order[-1]])
                    order.append(key)
                    sums[key] = scatter_wt(ready[key])
                    started.append(sums[key])
            all_grads[layer] = grads
            return value

        return pin

    def beside_of(layer):
        def aside(point, step, grads):
            wanted = beside.get((layer, point), ())
            value, extra = step([grads[name][at] for name, at in wanted])
            for (name, at), result in zip(wanted, extra):
                dots[(name, layer), at] = result
            return value

        return aside

    all_grads = {}
    vector_grads = [None, None]
    for layer in (1, 0):
        coming, vector_grads[layer] = backward_layer(
            coming,
            plan.gathered(coming),
            kept[layer],
            functools.partial(weight, layer),
            vectors[layer],
            plan,
            place,
            block,
            backward_pin(layer),
            beside_of(layer),
        )

    def to_owner(name):
        there = swap(jnp.where(first, sums[name, 1], sums[name, 0]), SECTION)
        return jnp.where(first, sums[name, 0], sums[name, 1]), there

    sent[QKV, 0], coming = tied(sent[QKV, 0], coming)
    ready[QKV, 0] = add((QKV, 0), None)
    sums[QKV, 0] = scatter_wt(after(ready[QKV, 0], sums[FC, 0]))
    fc_own, fc_there = to_owner(FC)
    fc_halves = (jnp.where(first, fc_own, fc_there), jnp.where(first, fc_there, fc_own))
    fc_parts = [gathered(value, CTX) for value in fc_halves]
    leaving = state([coming], [fc_there])
    sums[PROJ, 0] = scatter_wt(after(ready[PROJ, 0], sums[QKV, 0]))

    def packed(grads):
        def placed(piece):
            zeros = jnp.zeros((plan.padded,), jnp.float32)
            return lax.dynamic_update_slice_in_dim(zeros, piece, ci * plan.step, 0)[:width]

        full = jnp.stack(
            [
                grads["attn_gain"],
                grads["attn_shift"],
                placed(grads["qkv"][:span]),
                placed(grads["qkv"][2 * span :]),
                grads["proj"],
                grads["mlp_gain"],
                grads["mlp_shift"],
                grads["out"],
            ]
        )
        full = jnp.swapaxes(full.reshape(8, owners, shard), 0, 1).reshape(owners, 8 * shard)
        halves = [piece.reshape(owners, half) for piece in grads["fc"]]
        halves = jnp.where(
            first, jnp.concatenate(halves, 1), jnp.concatenate(halves[::-1], 1)
        )
        zeros = jnp.zeros((owners, hidden_rows), jnp.float32)
        return jnp.concatenate(
            [full, lax.dynamic_update_slice_in_dim(zeros, halves, ci * part, 1)], 1
        )

    late, early = packed(vector_grads[0]), packed(vector_grads[1])
    early = after(early, leaving)
    total = jnp.where(first, late, early) + swap(jnp.where(first, early, late), SECTION)
    for bit in bits_of(CTX):
        total = total + swap(total, CTX, bit)
    pieces = {
        at: lax.dynamic_index_in_dim(total, plan.wi ^ at, 0, keepdims=False) for at in range(owners)
    }
    for bit in bits_of(WT):
        for at in sorted(pieces, reverse=True):
            if at & bit:
                pieces[at ^ bit] = pieces[at ^ bit] + swap(pieces.pop(at), WT, bit)
    total = pieces[0]
    vector_out = total[: 8 * shard].reshape(8, shard)
    fc_bias_out = total[8 * shard :]

    stays = jnp.where(first, coming, leaving)
    came = swap(jnp.where(first, leaving, coming), SECTION)
    result = jnp.where(first, jnp.stack([stays, came]), jnp.stack([came, stays]))
    result = result.reshape(1, 2, 1, rows, width)
    result = after(result, *jax.tree.leaves(started))
    out_grad = joined_rows(owned[OUT], ci)
    segments = [
        (kind, owner, at * half, at * hidden_rows + owner * part + kind * half, half)
        for at in range(owners)
        for owner in range(count)
        for kind in range(2)
    ]
    fc_grad = joined_columns(fc_parts, segments, ci, owners * hidden_rows)
    qkv_own, qkv_there = to_owner(QKV)
    qkv_halves = [jnp.where(first, qkv_own, qkv_there), jnp.where(first, qkv_there, qkv_own)]
    qkv_parts = gathered(jnp.concatenate(qkv_halves), CTX)
    segments = [
        (
            0,
            owner,
            at * span,
            at * width + owner * plan.step,
            plan.step if owner < count - 1 else width - plan.step * (count - 1),
        )
        for at in range(3)
        for owner in range(count)
    ]
    qkv_grad = joined_columns([qkv_parts], segments, ci, 3 * width)
    proj_own, proj_there = to_owner(PROJ)
    proj_parts = gathered(low(wide(proj_own) + wide(proj_there)), CTX)
    starts = [plan.proj_start(ci ^ at) for at in range(count)]
    proj_grad = placed_rows(proj_parts, starts, 1, shard, jnp.float32)

    return (
        result,
        vector_out[0][None],
        vector_out[1][None],
        qkv_grad[None],
        vector_out[2][None],
        vector_out[3][None],
        proj_grad[None],
        vector_out[4][None],
        vector_out[5][None],
        vector_out[6][None],
        fc_grad[None],
        fc_bias_out[None],
        out_grad[None],
        vector_out[7][None],
    )


def solution(mesh):
    return jax.shard_map(
        body,
        mesh=mesh,
        in_specs=(
            P(SECTION, None, WT, CTX, None),
            P(),
            P(SECTION, WT),
            P(SECTION, WT),
            P(SECTION, WT, None),
            P(SECTION, WT),
            P(SECTION, WT),
            P(SECTION, WT, None),
            P(SECTION, WT),
            P(SECTION, WT),
            P(SECTION, WT),
            P(SECTION, WT, None),
            P(SECTION, WT),
            P(SECTION, WT, None),
            P(SECTION, WT),
        ),
        out_specs=(
            P(SECTION, None, WT, CTX, None),
            P(SECTION, WT),
            P(SECTION, WT),
            P(SECTION, WT, None),
            P(SECTION, WT),
            P(SECTION, WT),
            P(SECTION, WT, None),
            P(SECTION, WT),
            P(SECTION, WT),
            P(SECTION, WT),
            P(SECTION, WT, None),
            P(SECTION, WT),
            P(SECTION, WT, None),
            P(SECTION, WT),
        ),
        check_vma=False,
    )
```

```python
import functools
import math

import jax
import jax.numpy as jnp
from jax import lax
from jax.experimental import pallas as pl
from jax.experimental.pallas import tpu as pltpu
from jax.sharding import PartitionSpec as P

SECTION, CTX, WT = "section", "ctx", "wt"
QKV, PROJ, FC, OUT = range(4)
OWN, NORM, SCORES, MIXED, GATHERED, ACTIVE, RESULT = range(7)
START, HIDDEN, SECOND, SUM, HEADS, BACK, THERE, FIRST, END = range(9)
FULL, MOVED, SEND, CAME, REDUCE, DONE, HOP, OWNED, TOKEN = range(9)

HEAD_DIM = 64
NEG = -1000000000.0
LANES = 128


def nt_dot(left, right):
    return lax.dot_general(left, right, (((1,), (1,)), ((), ())), preferred_element_type=jnp.float32)


def nn_dot(left, right):
    return jnp.dot(left, right, preferred_element_type=jnp.float32)


def causal_scores(keys, query, tile):
    scores = nt_dot(keys, query)
    edge = scores.shape[0] - tile
    key_at = lax.broadcasted_iota(jnp.int32, (tile, tile), 0)
    query_at = lax.broadcasted_iota(jnp.int32, (tile, tile), 1)
    last = jnp.where(key_at <= query_at, scores[edge:], NEG)
    return jnp.concatenate([scores[:edge], last], 0) if edge else last


def attend_kernel(block, tile, heads, place, qkv, out, log_total, query, keyed, valued, mixed):
    length, three = qkv.shape
    span = three // 3
    lane = lax.broadcasted_iota(jnp.int32, (tile, LANES), 1)

    def pair(index, carry):
        start = pl.multiple_of(index * LANES, LANES)
        for at in range(length // block):
            rows = pl.ds(pl.multiple_of(place[at] * block, block), block)
            here = pl.ds(at * block, block)
            query[here, :] = qkv[rows, pl.ds(start, LANES)] * (HEAD_DIM ** (-0.5))
            keyed[here, :] = qkv[rows, pl.ds(span + start, LANES)]
            valued[:, here] = qkv[rows, pl.ds(2 * span + start, LANES)].T

        for half in range(2):

            @pl.when(2 * index + half < heads)
            def _():
                mine = (lane < HEAD_DIM) if half == 0 else (lane >= HEAD_DIM)
                features = slice(half * HEAD_DIM, (half + 1) * HEAD_DIM)
                for at in range(length // tile):
                    seen = (at + 1) * tile
                    cols = slice(at * tile, seen)
                    part = jnp.where(mine, query[cols, :], 0)
                    scores = causal_scores(keyed[:seen, :], part, tile)
                    highest = jnp.max(scores, 0, keepdims=True)
                    exponent = jnp.exp(scores - highest)
                    total = jnp.sum(exponent, 0, keepdims=True)
                    result = nn_dot(valued[features, :seen], exponent.astype(jnp.bfloat16))
                    mixed[features, cols] = result * (1.0 / total)
                    log_total[pl.ds(2 * index + half, 1), cols] = highest + jnp.log(total)

        for at in range(length // block):
            rows = pl.ds(pl.multiple_of(place[at] * block, block), block)
            out[rows, pl.ds(start, LANES)] = mixed[:, at * block : (at + 1) * block].T.astype(out.dtype)
        return carry

    mixed[...] = jnp.zeros_like(mixed)
    lax.fori_loop(0, span // LANES, pair, 0)


def attend(place, qkv, heads, block):
    length, three = qkv.shape
    span = three // 3
    tile = min(256, length)
    rows = -(-span // HEAD_DIM // 8) * 8
    vmem = pl.BlockSpec(memory_space=pltpu.VMEM)
    return pl.pallas_call(
        functools.partial(attend_kernel, block, tile, heads),
        out_shape=(
            jax.ShapeDtypeStruct((length, span), jnp.bfloat16),
            jax.ShapeDtypeStruct((rows, length), jnp.float32),
        ),
        in_specs=[pl.BlockSpec(memory_space=pltpu.SMEM), vmem],
        out_specs=(vmem, vmem),
        scratch_shapes=[
            pltpu.VMEM((length, LANES), jnp.bfloat16),
            pltpu.VMEM((length, LANES), jnp.bfloat16),
            pltpu.VMEM((LANES, length), jnp.bfloat16),
            pltpu.VMEM((LANES, length), jnp.float32),
        ],
        compiler_params=pltpu.CompilerParams(vmem_limit_bytes=40 * 1024 * 1024),
        cost_estimate=pl.CostEstimate(
            flops=0, bytes_accessed=0, transcendentals=0
        ),
    )(place, qkv)


def attend_back_kernel(
    block, tile, heads, place, qkv, grad_mixed, log_total, out,
    query, keyed, keyed_t, valued, grad, grad_query, grad_key, grad_value,
):
    length, three = qkv.shape
    span = three // 3
    scale = HEAD_DIM ** (-0.5)
    lane = lax.broadcasted_iota(jnp.int32, (tile, LANES), 1)

    def pair(index, carry):
        start = pl.multiple_of(index * LANES, LANES)
        for at in range(length // block):
            rows = pl.ds(pl.multiple_of(place[at] * block, block), block)
            here = pl.ds(at * block, block)
            query[here, :] = qkv[rows, pl.ds(start, LANES)] * scale
            key_part = qkv[rows, pl.ds(span + start, LANES)]
            keyed[here, :] = key_part
            keyed_t[:, here] = key_part.T
            valued[here, :] = qkv[rows, pl.ds(2 * span + start, LANES)]
            grad[here, :] = grad_mixed[rows, pl.ds(start, LANES)]
        grad_query[...] = jnp.zeros_like(grad_query)
        grad_key[...] = jnp.zeros_like(grad_key)
        grad_value[...] = jnp.zeros_like(grad_value)

        for half in range(2):

            @pl.when(2 * index + half < heads)
            def _():
                mine = (lane < HEAD_DIM) if half == 0 else (lane >= HEAD_DIM)
                features = slice(half * HEAD_DIM, (half + 1) * HEAD_DIM)
                for at in range(length // tile):
                    seen = (at + 1) * tile
                    cols = slice(at * tile, seen)
                    part = jnp.where(mine, query[cols, :], 0)
                    grad_part = jnp.where(mine, grad[cols, :], 0)
                    scores = causal_scores(keyed[:seen, :], part, tile)
                    chance = jnp.exp(scores - log_total[pl.ds(2 * index + half, 1), cols])
                    grad_chance = nt_dot(valued[:seen, :], grad_part)
                    inner = jnp.sum(chance * grad_chance, 0, keepdims=True)
                    grad_scores = (chance * (grad_chance - inner)).astype(jnp.bfloat16)
                    grad_value[:seen, :] += nn_dot(chance.astype(jnp.bfloat16), grad_part)
                    grad_key[:seen, :] += nn_dot(grad_scores, part)
                    grad_query[features, cols] = nn_dot(keyed_t[features, :seen], grad_scores) * scale

        for at in range(length // block):
            rows = pl.ds(pl.multiple_of(place[at] * block, block), block)
            here = slice(at * block, (at + 1) * block)
            out[rows, pl.ds(start, LANES)] = grad_query[:, here].T.astype(out.dtype)
            out[rows, pl.ds(span + start, LANES)] = grad_key[here, :].astype(out.dtype)
            out[rows, pl.ds(2 * span + start, LANES)] = grad_value[here, :].astype(out.dtype)
        return carry

    lax.fori_loop(0, span // LANES, pair, 0)


def attend_back(place, qkv, grad_mixed, log_total, heads, block):
    length, three = qkv.shape
    span = three // 3
    tile = min(256, length)
    vmem = pl.BlockSpec(memory_space=pltpu.VMEM)
    return pl.pallas_call(
        functools.partial(attend_back_kernel, block, tile, heads),
        out_shape=jax.ShapeDtypeStruct((length, three), jnp.bfloat16),
        in_specs=[pl.BlockSpec(memory_space=pltpu.SMEM), vmem, vmem, vmem],
        out_specs=vmem,
        scratch_shapes=[
            pltpu.VMEM((length, LANES), jnp.bfloat16),
            pltpu.VMEM((length, LANES), jnp.bfloat16),
            pltpu.VMEM((LANES, length), jnp.bfloat16),
            pltpu.VMEM((length, LANES), jnp.bfloat16),
            pltpu.VMEM((length, LANES), jnp.bfloat16),
            pltpu.VMEM((LANES, length), jnp.float32),
            pltpu.VMEM((length, LANES), jnp.float32),
            pltpu.VMEM((length, LANES), jnp.float32),
        ],
        compiler_params=pltpu.CompilerParams(vmem_limit_bytes=48 * 1024 * 1024),
        cost_estimate=pl.CostEstimate(
            flops=0, bytes_accessed=0, transcendentals=0
        ),
    )(place, qkv, grad_mixed, log_total)


EPS = 1e-05
GELU_A = math.sqrt(2.0 / math.pi)
GELU_B = 0.044715


def flip(axis, bit):
    return [(at, at ^ bit) for at in range(lax.axis_size(axis))]


def swap(value, axis, bit=1):
    return lax.ppermute(value, axis, flip(axis, bit))


def bits_of(axis):
    bits, bit = [], 1
    while bit < lax.axis_size(axis):
        bits.append(bit)
        bit *= 2
    return bits


def gathered(value, axis):
    pieces = {0: value}
    for bit in reversed(bits_of(axis)):
        for at in list(pieces):
            pieces[at | bit] = swap(pieces[at], axis, bit)
    return [pieces[at] for at in range(lax.axis_size(axis))]


def gathered_whole(value, axis):
    pieces = {0: value}
    for bit in reversed(bits_of(axis)):
        held = list(pieces)
        for at, came in zip(held, together([pieces[at] for at in held], axis, bit)):
            pieces[at | bit] = came
    return [pieces[at] for at in range(lax.axis_size(axis))]


def together(pieces, axis, bit):
    if len(pieces) == 1:
        return [swap(pieces[0], axis, bit)]
    came = swap(jnp.concatenate(pieces), axis, bit)
    rows = pieces[0].shape[0]
    return [came[at * rows : (at + 1) * rows] for at in range(len(pieces))]


def summed(pieces, axis, bits=None):
    pieces = dict(pieces) if isinstance(pieces, dict) else dict(enumerate(pieces))
    for bit in bits_of(axis) if bits is None else bits:
        for at in sorted(pieces, reverse=True):
            if at & bit:
                came = swap(pieces.pop(at).astype(jnp.bfloat16), axis, bit)
                pieces[at ^ bit] = pieces[at ^ bit].astype(jnp.float32) + came.astype(jnp.float32)
    return pieces[0] if len(pieces) == 1 else pieces


def exchanged(pieces, axis):
    return [swap(piece, axis, at) if at else piece for at, piece in enumerate(pieces)]


def at_once(go, step, operands, aside=None):
    aside = aside or []
    counts = [len(inputs) for unused, inputs in aside]

    def both(operands, inputs):
        results, at = [], 0
        for (work, unused), count in zip(aside, counts):
            results.append(work(*inputs[at : at + count]))
            at += count
        return step(*operands), results

    inputs = [value for unused, values in aside for value in values]
    shapes = jax.eval_shape(both, operands, inputs)

    def nothing(*unused):
        return jax.tree.map(lambda shape: jnp.zeros(shape.shape, shape.dtype), shapes)

    return lax.cond(go, both, nothing, operands, inputs)


def by_owner(pieces, axis):
    here = lax.axis_index(axis)
    whole = jnp.zeros((len(pieces),) + pieces[0].shape, pieces[0].dtype)
    for at, piece in enumerate(pieces):
        whole = lax.dynamic_update_index_in_dim(whole, piece, here ^ at, 0)
    return whole


def after(value, *marks):
    return lax.optimization_barrier(marks + (value,))[-1]


def tied(*values):
    return lax.optimization_barrier(values)


def over_wt(value, tiled=True):
    return lax.all_gather(value, WT, axis=0, tiled=tiled)


def scatter_wt(value, tiled=True):
    return lax.psum_scatter(value, WT, scatter_dimension=0, tiled=tiled)


def dot(left, right):
    return jnp.dot(left, right, preferred_element_type=jnp.float32)


def dot_nt(left, right):
    return lax.dot_general(left, right, (((1,), (1,)), ((), ())), preferred_element_type=jnp.float32)


def dot_tn(left, right):
    return lax.dot_general(left, right, (((0,), (0,)), ((), ())), preferred_element_type=jnp.float32)


def low(value):
    return value.astype(jnp.bfloat16)


def wide(value):
    return value.astype(jnp.float32)


def normed(values):
    center = values - jnp.mean(values, -1, keepdims=True)
    rate = lax.rsqrt(jnp.mean(center * center, -1, keepdims=True) + EPS)
    return center * rate, rate


def norm_back(grad, gain, values):
    unit, rate = normed(values)
    inner = grad * gain
    back = (
        inner
        - jnp.mean(inner, -1, keepdims=True)
        - unit * jnp.mean(inner * unit, -1, keepdims=True)
    ) * rate
    return back, jnp.sum(grad * unit, 0), jnp.sum(grad, 0)


def gelu(value):
    return 0.5 * value * (1.0 + jnp.tanh(GELU_A * (value + GELU_B * value * value * value)))


def gelu_slope(value):
    square = value * value
    bend = jnp.tanh(GELU_A * (value + GELU_B * value * square))
    return 0.5 * (1.0 + bend) + 0.5 * value * (1.0 - bend * bend) * (
        GELU_A * (1.0 + 3.0 * GELU_B * square)
    )


def joined_kernel(count, segments, at, *refs):
    out, pieces = refs[-1], refs[:-1]
    kinds = len(pieces) // count
    picked = {}
    for kind, owner, source, target, columns in segments:
        if (kind, owner) not in picked:
            value = pieces[kind * count][...].astype(jnp.float32)
            for step in range(1, count):
                other = pieces[kind * count + step][...].astype(jnp.float32)
                value = jnp.where((at[0] ^ owner) == step, other, value)
            picked[kind, owner] = value
        out[:, target : target + columns] = picked[kind, owner][:, source : source + columns]
    assert kinds * count == len(pieces)


def joined_columns(pieces, segments, ci, columns):
    flat = [piece for kind in pieces for piece in kind]
    rows = flat[0].shape[0]
    tile = 80 if rows % 80 == 0 else rows
    return pl.pallas_call(
        functools.partial(joined_kernel, len(pieces[0]), segments),
        out_shape=jax.ShapeDtypeStruct((rows, columns), jnp.float32),
        grid=(rows // tile,),
        in_specs=[pl.BlockSpec(memory_space=pltpu.SMEM)]
        + [pl.BlockSpec((tile, piece.shape[1]), lambda at: (at, 0)) for piece in flat],
        out_specs=pl.BlockSpec((tile, columns), lambda at: (at, 0)),
        compiler_params=pltpu.CompilerParams(vmem_limit_bytes=48 * 1024 * 1024),
        cost_estimate=pl.CostEstimate(
            flops=0, bytes_accessed=6 * rows * columns, transcendentals=0
        ),
    )(ci.reshape(1), *flat)


class Plan:
    def __init__(self, width, hidden_rows, go):
        self.go = go
        self.count = lax.axis_size(CTX)
        self.ci = lax.axis_index(CTX)
        self.first = lax.axis_index(SECTION) == 0
        self.xi = lax.axis_index(SECTION)
        self.wi = lax.axis_index(WT)
        self.width = width
        heads = width // HEAD_DIM
        stride = heads // self.count
        self.heads = heads - stride * (self.count - 1)
        self.step = stride * HEAD_DIM
        self.span = (self.heads + self.heads % 2) * HEAD_DIM
        self.padded = self.step * (self.count - 1) + self.span
        self.owned = jnp.where(self.ci == self.count - 1, self.heads, stride) * HEAD_DIM
        self.part = hidden_rows // self.count
        self.half = self.part // 2
        self.shard = width // lax.axis_size(WT)
        self.proj_rows = -(-self.shard // self.count // 16) * 16

    def proj_start(self, index):
        return jnp.minimum(index * self.proj_rows, self.shard - self.proj_rows)

    def gathered(self, value):
        def step(value):
            return gathered(value, CTX)[1:]

        return [value] + at_once(self.go, step, [value])[0]

    def exchanged(self, pieces, aside=None):
        def step(*pieces):
            return [swap(piece, CTX, at + 1) for at, piece in enumerate(pieces)]

        came, extra = at_once(self.go, step, pieces[1:], aside)
        return pieces[:1] + came, extra

    def summed(self, value, aside=None):
        def step(value):
            return wide(summed(cut(value, self.count), CTX))

        return at_once(self.go, step, [value], aside)

    def proj_parts(self, left, right):
        parts = grad_dot(left, right).reshape(-1, self.shard, self.width)
        return [
            lax.dynamic_slice_in_dim(parts, self.proj_start(self.ci ^ at), self.proj_rows, 1)
            for at in range(self.count)
        ]

    def padded_out(self, array):
        return jnp.pad(array, [(0, 0)] * (array.ndim - 1) + [(0, self.padded - array.shape[-1])])

    def window(self, padded, index):
        return lax.dynamic_slice_in_dim(padded, index * self.step, self.span, padded.ndim - 1)

    def joined(self, ordered):
        last = self.width - self.step * (self.count - 1)
        parts = [ordered[at, ..., : self.step] for at in range(self.count - 1)]
        return jnp.concatenate(parts + [ordered[self.count - 1, ..., :last]], -1)


def joined_rows_kernel(at, *refs):
    out, pieces = refs[-1], refs[:-1]
    step = pl.program_id(0)
    for index, piece in enumerate(pieces):

        @pl.when(step == index)
        def _():
            out[...] = piece[...].astype(jnp.float32)


def joined_rows(pieces, ci):
    rows, columns = pieces[0].shape
    count = len(pieces)
    if rows % 8:
        return wide(by_owner(pieces, CTX)).reshape(count * rows, columns)
    return pl.pallas_call(
        joined_rows_kernel,
        out_shape=jax.ShapeDtypeStruct((count * rows, columns), jnp.float32),
        grid_spec=pltpu.PrefetchScalarGridSpec(
            num_scalar_prefetch=1,
            grid=(count,),
            in_specs=[pl.BlockSpec((rows, columns), lambda step, at: (0, 0))] * count,
            out_specs=pl.BlockSpec((rows, columns), lambda step, at: (at[0] ^ step, 0)),
        ),
        compiler_params=pltpu.CompilerParams(vmem_limit_bytes=48 * 1024 * 1024),
        cost_estimate=pl.CostEstimate(
            flops=0, bytes_accessed=6 * count * rows * columns, transcendentals=0
        ),
    )(ci.reshape(1), *pieces)


def placed_kernel(owners, start, *refs):
    out, pieces = refs[-1], refs[:-1]
    rows = pieces[0].shape[0] // owners
    shard = out.shape[0] // owners
    for at, piece in enumerate(pieces):
        for owner in range(owners):
            here = pl.ds(pl.multiple_of(owner * shard + start[at], 16), rows)
            out[here, :] = piece[owner * rows : (owner + 1) * rows, :].astype(out.dtype)


def placed_rows(pieces, starts, owners, shard, dtype):
    columns = pieces[0].shape[1]
    vmem = pl.BlockSpec(memory_space=pltpu.VMEM)
    return pl.pallas_call(
        functools.partial(placed_kernel, owners),
        out_shape=jax.ShapeDtypeStruct((owners * shard, columns), dtype),
        in_specs=[pl.BlockSpec(memory_space=pltpu.SMEM)] + [vmem] * len(pieces),
        out_specs=vmem,
        compiler_params=pltpu.CompilerParams(vmem_limit_bytes=48 * 1024 * 1024),
        cost_estimate=pl.CostEstimate(
            flops=0, bytes_accessed=4 * owners * shard * columns, transcendentals=0
        ),
    )(jnp.stack(starts), *pieces)


def cut(value, count):
    rows = value.shape[0] // count
    return [value[at * rows : (at + 1) * rows] for at in range(count)]


def forward_layer(entering, weight, vectors, plan, place, block, pin):
    attn_gain, attn_shift, bias_qkv, proj_bias, mlp_gain, mlp_shift, fc_bias, out_bias = vectors
    stream = wide(entering)
    first_norm = pin(OWN, low(normed(stream)[0] * attn_gain + attn_shift))
    first_norm = jnp.concatenate(pin(NORM, plan.gathered(first_norm)))
    qkv = pin(SCORES, low(dot(first_norm, weight(QKV)) + bias_qkv))
    mixed, log_total = attend(place, qkv, plan.heads, block)
    mixed = pin(MIXED, mixed)
    mixed_all = plan.joined(by_owner(plan.exchanged(cut(mixed, plan.count))[0], CTX))
    middle = (dot(mixed_all, weight(PROJ)) + proj_bias) + stream
    second_norm = low(normed(middle)[0] * mlp_gain + mlp_shift)
    second_norm = jnp.concatenate(pin(GATHERED, plan.gathered(second_norm)))
    hidden = [dot(second_norm, part) + bias for part, bias in zip(weight(FC), fc_bias)]
    active = pin(ACTIVE, [low(gelu(part)) for part in hidden])

    def final(first_marks=(), last_marks=()):
        parts = after(active, *first_marks)
        w_out = weight(OUT)
        result = pin(RESULT, low(dot(parts[0], w_out[0]) + dot(parts[1], w_out[1])))
        return low((plan.summed(after(result, *last_marks))[0] + out_bias) + middle)

    kept = (stream, first_norm, qkv, log_total, mixed_all, middle, second_norm, hidden, active)
    return final, kept


def grad_dot(left, right):
    return low(dot_tn(left, right))


def grad_dot_all(left, *right):
    return low(dot_tn(left, jnp.concatenate(right)))


def backward_layer(coming, coming_all, kept, weight, vectors, plan, place, block, pin, aside):
    attn_gain, attn_shift, bias_qkv, proj_bias, mlp_gain, mlp_shift, fc_bias, out_bias = vectors
    stream, first_norm, qkv, log_total, mixed_all, middle, second_norm, hidden, active = kept
    grads, sums = {}, {}
    w_fc, w_out = weight(FC), weight(OUT)
    grads[OUT] = [(grad_dot_all, [part] + coming_all) for part in active]
    coming_all = pin(START, coming_all, grads)
    grads[OUT] = [(grad_dot_all, [part] + coming_all) for part in active]
    coming_whole = jnp.concatenate(coming_all)
    grad_hidden = [
        low(dot_nt(coming_whole, part) * gelu_slope(at)) for part, at in zip(w_out, hidden)
    ]
    grads[FC] = [(grad_dot, [second_norm, part]) for part in grad_hidden]
    grad_hidden = pin(HIDDEN, grad_hidden, grads)
    grads[FC] = [(grad_dot, [second_norm, part]) for part in grad_hidden]
    grad_second = low(dot_nt(grad_hidden[0], w_fc[0]) + dot_nt(grad_hidden[1], w_fc[1]))
    grad_second = pin(SECOND, grad_second, grads)
    grad_norm = aside(SUM, lambda extra: plan.summed(grad_second, extra), grads)
    grad_norm = pin(SUM, grad_norm, grads)
    back, sums["mlp_gain"], sums["mlp_shift"] = norm_back(grad_norm, mlp_gain, middle)
    grad_final = wide(coming)
    grad_middle = back + grad_final
    branch = low(grad_middle)
    grad_mixed = plan.padded_out(low(dot_nt(branch, weight(PROJ))))
    pieces = [plan.window(grad_mixed, plan.ci ^ at) for at in range(plan.count)]
    grads[PROJ] = [(plan.proj_parts, [mixed_all, branch])]
    grad_heads = aside(HEADS, lambda extra: plan.exchanged(pieces, extra), grads)
    grad_heads = jnp.concatenate(grad_heads)
    column = lax.broadcasted_iota(jnp.int32, grad_heads.shape, 1)
    grad_heads = pin(HEADS, jnp.where(column < plan.owned, grad_heads, 0), grads)
    grad_qkv = attend_back(place, qkv, grad_heads, log_total, plan.heads, block)
    grad_qkv = pin(BACK, grad_qkv, grads)
    grads[QKV] = [(grad_dot, [first_norm, grad_qkv])]
    grad_qkv = pin(THERE, grad_qkv, grads)
    grad_first = pin(FIRST, low(dot_nt(grad_qkv, weight(QKV))), grads)
    grad_norm = aside(END, lambda extra: plan.summed(grad_first, extra), grads)
    grad_norm = pin(END, grad_norm, grads)
    back, sums["attn_gain"], sums["attn_shift"] = norm_back(grad_norm, attn_gain, stream)
    leaving = low(back + grad_middle)
    sums["fc"] = [jnp.sum(wide(part), 0) for part in grad_hidden]
    sums["out"] = jnp.sum(grad_final, 0)
    sums["proj"] = jnp.sum(wide(branch), 0)
    sums["qkv"] = jnp.sum(wide(grad_qkv), 0)
    return leaving, sums


def body(
    feed,
    block_order,
    attn_gain,
    attn_shift,
    w_qkv,
    query_bias,
    value_bias,
    w_proj,
    proj_bias,
    mlp_gain,
    mlp_shift,
    w_fc,
    fc_bias,
    w_out,
    out_bias,
):
    width = w_proj.shape[2]
    shard = w_proj.shape[1]
    hidden_rows = w_out.shape[1]
    plan = Plan(width, hidden_rows, block_order[0] >= 0)
    count, owners = plan.count, lax.axis_size(WT)
    first, xi, ci = plan.first, plan.xi, plan.ci
    part, half, span = plan.part, plan.half, plan.span
    rows = feed.shape[3]
    block = rows // 2

    def mine_other(mine, other):
        return (jnp.where(first, mine, other), jnp.where(first, other, mine))

    slots = jnp.arange(2 * count, dtype=jnp.int32)
    held = 2 * (ci ^ (slots // 2)) + slots % 2
    table = (held[:, None] == slots[None, :]).astype(jnp.int32)
    blocks_held = jnp.sum(table * block_order[None, :], 1)
    found = (blocks_held[None, :] == slots[:, None]).astype(jnp.int32)
    place = jnp.sum(found * slots[None, :], 1)

    fc_part = lax.dynamic_slice_in_dim(fc_bias[0], ci * part, part, 0)
    names = (attn_gain, attn_shift, query_bias, value_bias, proj_bias, mlp_gain, mlp_shift, out_bias)
    small = jnp.concatenate([vector[0] for vector in names] + [fc_part])
    local = feed[0, :, 0]
    feed_own = lax.dynamic_index_in_dim(local, xi, 0, keepdims=False)
    feed_gone = lax.dynamic_index_in_dim(local, 1 - xi, 0, keepdims=False)

    def fc_shard(duty):
        return jnp.concatenate(
            [
                lax.dynamic_slice_in_dim(
                    w_fc[0], owner * hidden_rows + ci * part + duty * half, half, 1
                )
                for owner in range(owners)
            ],
            1,
        )

    def out_shard(duty):
        return lax.dynamic_slice_in_dim(w_out[0], ci * part + duty * half, half, 0)

    qkv_shard = jnp.concatenate(
        [
            plan.window(plan.padded_out(w_qkv[0][:, at * width : (at + 1) * width]), ci)
            for at in range(3)
        ],
        1,
    )
    proj_shard = lax.dynamic_slice_in_dim(w_proj[0], plan.proj_start(ci), plan.proj_rows, 0)

    def qkv_half(duty):
        return lax.dynamic_slice_in_dim(qkv_shard, duty * (shard // 2), shard // 2, 0)

    whole_here = {(OUT, 1)}
    own_shards = {QKV: qkv_half(xi), PROJ: proj_shard, FC: fc_shard(xi), OUT: out_shard(xi)}
    gone = {QKV: qkv_half(1 - xi), PROJ: proj_shard, FC: fc_shard(1 - xi), OUT: out_shard(1 - xi)}
    came = {QKV: swap(gone[QKV], SECTION)}
    started = [came[QKV]]
    feed_gone = after(feed_gone, gone[QKV])
    feed_came = swap(feed_gone, SECTION)
    small_came = swap(after(small, feed_gone), SECTION)
    started += [feed_came, small_came]
    before = feed_gone
    for name in (PROJ, FC, OUT):
        before = after(gone[name], before)
        came[name] = swap(before, SECTION)
        started.append(came[name])
    shards = {name: mine_other(own_shards[name], came[name]) for name in (QKV, PROJ)}
    last_gone = after(own_shards[OUT], before)
    last_came = swap(last_gone, SECTION)

    entering, coming = mine_other(feed_own, feed_came)
    small = jnp.stack(mine_other(small, small_came))
    small = wide(by_owner(gathered(small, WT), WT))

    def vectors_of(layer):
        full = jnp.swapaxes(small[:, layer, : 8 * shard].reshape(owners, 8, shard), 0, 1)
        full = full.reshape(8, owners * shard)
        hidden = small[:, layer, 8 * shard :]
        halves = [
            lax.dynamic_slice_in_dim(hidden, duty * half, half, 1).reshape(-1) for duty in (xi, 1 - xi)
        ]
        query = plan.window(plan.padded_out(full[2]), ci)
        value = plan.window(plan.padded_out(full[3]), ci)
        bias_qkv = jnp.concatenate([query, jnp.zeros_like(query), value])
        return (full[0], full[1], bias_qkv, full[4], full[5], full[6], halves, full[7])

    vectors = [vectors_of(layer) for layer in range(2)]
    full, operands = {}, []
    tiny = small_came[:128]

    def gather_over_wt(keys, *marks):
        for key in keys:
            name, layer = key
            piece = after(shards[name][layer], *operands[-1:], *marks)
            operands.append(piece)
            full[key] = over_wt(piece)
            started.append(full[key])

    gather_over_wt([(QKV, 0)])
    gather_over_wt([(PROJ, 0)], feed_came, small_came)

    made, moved = {}, {}

    def move(key):
        if key not in moved:
            value = full[key]
            if key[0] == PROJ:
                moved[key] = gathered(value, CTX)
            elif key in whole_here:
                moved[key] = None
            else:
                moved[key] = swap(value, SECTION)
            started.append(moved[key])
        return moved[key]

    def weight(layer, name):
        key = (name, layer)
        if key in made:
            return made[key]
        other, value = move(key), full[key]
        if name == QKV:
            halves = [part.reshape(owners, shard // 2, 3 * span) for part in mine_other(value, other)]
            result = jnp.stack(halves, 1).reshape(width, 3 * span)
        elif name == PROJ:
            starts = [plan.proj_start(ci ^ at) for at in range(count)]
            result = placed_rows(other, starts, owners, shard, jnp.bfloat16)
        elif key in whole_here:
            result = tuple(value[:, at].reshape(-1, value.shape[-1]) for at in range(2))
        else:
            result = (value, other)
        made[key] = result
        return result

    front = {
        (0, OWN): ((FULL, QKV, 0),),
        (0, NORM): ((FULL, PROJ, 0),),
        (0, MIXED): ((MOVED, PROJ, 0), (FULL, FC, 0)),
        (0, GATHERED): ((MOVED, FC, 0), (FULL, OUT, 0)),
        (0, ACTIVE): ((FULL, PROJ, 1),),
        (0, RESULT): ((MOVED, PROJ, 1), (FULL, QKV, 1)),
        (1, NORM): ((MOVED, QKV, 1), (FULL, FC, 1), (TOKEN,)),
        (1, GATHERED): ((MOVED, FC, 1),),
    }

    coming_parts = []

    def forward_pin(layer):
        def pin(point, value):
            if (layer, point) == (0, OWN):
                for name in (FC, OUT):
                    shards[name] = mine_other(own_shards[name], after(came[name], value))
                keys = [(FC, 0), (OUT, 0), (PROJ, 1), (QKV, 1), (FC, 1)]
                gather_over_wt(keys, value)
            if (layer, point) == (0, MIXED):
                last, value = tied(last_came, value)
                shards[OUT, 1] = jnp.stack([shards[OUT][1], mine_other(gone[OUT], last)[1]])
            if (layer, point) == (0, ACTIVE):
                piece, value = tied(shards[OUT, 1], value)
                full[OUT, 1] = over_wt(after(piece, operands[-1]), tiled=False)
                started.append(full[OUT, 1])
            for kind, *key in front.get((layer, point), ()):
                key = tuple(key)
                if kind == TOKEN:
                    token, value = tied(tiny, value)
                    token, value = tied(swap(token, CTX), value)
                    started.append(token)
                elif kind == FULL:
                    full[key], value = tied(full[key], value)
                    move(key)
                else:
                    moved[key], value = tied(moved[key], value)
            if (layer, point) == (1, GATHERED):
                coming_parts.extend(gathered(after(coming, *value), CTX))
            return value

        return pin

    kept = []
    state = entering
    for layer in range(2):
        state, kept_here = forward_layer(
            state,
            functools.partial(weight, layer),
            vectors[layer],
            plan,
            place,
            block,
            forward_pin(layer),
        )
        kept.append(kept_here)
        if layer == 0:
            state = state()

    whole_sums = {(OUT, 1)}
    dots, sent, ready, sums, hops, order = {}, {}, {}, {}, {}, []

    def grad_of(key, at, grads):
        if (key, at) not in dots:
            work, inputs = grads[key[0]][at]
            dots[key, at] = work(*inputs)
        return dots[key, at]

    def prepared(key, grads):
        if key[0] == QKV:
            parts = grad_of(key, 0, grads).reshape(owners, 2, shard // 2, 3 * span)
            mine, away = (
                lax.dynamic_index_in_dim(parts, at, 1, keepdims=False).reshape(-1, 3 * span)
                for at in (xi, 1 - xi)
            )
            dots[key, QKV] = mine
            return away
        if key[0] == PROJ:
            return grad_of(key, 0, grads)
        if key in whole_sums:
            halves = [grad_of(key, at, grads).reshape(owners, half, width) for at in range(2)]
            return jnp.stack(halves, 1).reshape(-1, width)
        return grad_of(key, 1, grads)

    def core(*parts):
        return summed(parts, CTX, bits_of(CTX)[:-1])

    def start(key, away):
        if key[0] == PROJ:
            sent[key] = summed(away, CTX, bits_of(CTX)[-1:])
        elif key in whole_sums:
            sent[key] = away
        else:
            sent[key] = swap(away, SECTION)
        started.append(sent[key])

    def add(key, grads):
        came = sent[key]
        if key[0] == PROJ:
            return low(came).reshape(-1, width)
        if key in whole_sums:
            return came
        mine = dots[key, QKV] if key[0] == QKV else grad_of(key, 0, grads)
        return low(wide(came) + wide(mine))

    def hop(key):
        if key not in hops:
            hops[key] = lax.ppermute(sums[key], SECTION, [(1 - key[1], key[1])])
            started.append(hops[key])
        return hops[key]

    def both_halves(key):
        value, came = sums[key], hop(key)
        rows = value.shape[0]
        if key in whole_sums:
            rows = rows // 2
            own = low(wide(value[:rows]) + wide(came[rows:]))
            came = low(wide(value[rows:]) + wide(came[:rows]))
            value = own
        return (value, came) if key[1] == 0 else (came, value)

    def ordered(name):
        late, early = both_halves((name, 0)), both_halves((name, 1))
        return tuple(jnp.where(first, a, b) for a, b in zip(late, early))

    owned = {}
    back = {
        (1, START): ((SEND, OUT, 1), (CAME, OUT, 1), (REDUCE, OUT, 1)),
        (1, HIDDEN): ((SEND, FC, 1),),
        (1, HEADS): ((CAME, FC, 1), (SEND, PROJ, 1), (TOKEN,)),
        (1, BACK): ((DONE, OUT, 1), (REDUCE, FC, 1)),
        (1, FIRST): ((CAME, PROJ, 1),),
        (1, END): ((HOP, OUT, 1), (REDUCE, PROJ, 1), (SEND, QKV, 1), (TOKEN,)),
        (0, START): ((DONE, FC, 1), (SEND, OUT, 0)),
        (0, HIDDEN): ((CAME, QKV, 1),),
        (0, SECOND): ((REDUCE, QKV, 1),),
        (0, SUM): ((CAME, OUT, 0), (SEND, FC, 0), (TOKEN,), (DONE, PROJ, 1)),
        (0, HEADS): ((REDUCE, OUT, 0), (SEND, PROJ, 0), (TOKEN,)),
        (0, BACK): ((DONE, QKV, 1), (DONE, OUT, 0), (CAME, FC, 0), (REDUCE, FC, 0)),
        (0, THERE): ((SEND, QKV, 0), (TOKEN,), (HOP, OUT, 0)),
        (0, FIRST): ((CAME, PROJ, 0), (OWNED, OUT, 0)),
    }
    beside = {
        (1, HEADS): ((PROJ, 0),),
        (1, END): ((QKV, 0),),
        (0, SUM): ((OUT, 0),),
        (0, HEADS): ((PROJ, 0),),
    }

    def backward_pin(layer):
        def pin(point, value, grads):
            for kind, *key in back.get((layer, point), ()):
                key = tuple(key)
                if kind == SEND:
                    away = prepared(key, grads)
                    if key[0] == PROJ:
                        away = at_once(plan.go, core, away)[0]
                    away, value = tied(away, value)
                    start(key, away)
                elif kind == CAME:
                    sent[key], value = tied(sent[key], value)
                    ready[key] = add(key, grads if key[1] == layer else all_grads[key[1]])
                elif kind == TOKEN:
                    token, value = tied(tiny, value)
                    token, value = tied(swap(token, CTX), value)
                    started.append(token)
                elif kind == OWNED:
                    whole, value = tied(jnp.concatenate(ordered(key[0])), value)
                    owned[key[0]] = gathered_whole(whole, CTX)
                elif kind == HOP:
                    hops[key], value = tied(hop(key), value)
                elif kind == DONE:
                    sums[key], value = tied(sums[key], value)
                elif kind == REDUCE:
                    if order:
                        ready[key] = after(ready[key], ready[order[-1]])
                    order.append(key)
                    sums[key] = scatter_wt(ready[key])
                    started.append(sums[key])
            all_grads[layer] = grads
            return value

        return pin

    def beside_of(layer):
        def aside(point, step, grads):
            wanted = beside.get((layer, point), ())
            value, extra = step([grads[name][at] for name, at in wanted])
            for (name, at), result in zip(wanted, extra):
                dots[(name, layer), at] = result
            return value

        return aside

    all_grads = {}
    vector_grads = [None, None]
    for layer in (1, 0):
        coming, vector_grads[layer] = backward_layer(
            coming,
            coming_parts if layer else plan.gathered(coming),
            kept[layer],
            functools.partial(weight, layer),
            vectors[layer],
            plan,
            place,
            block,
            backward_pin(layer),
            beside_of(layer),
        )

    def to_owner(name):
        there = swap(jnp.where(first, sums[name, 1], sums[name, 0]), SECTION)
        return jnp.where(first, sums[name, 0], sums[name, 1]), there

    fc_away, coming = tied(jnp.where(first, sums[FC, 1], sums[FC, 0]), coming)
    fc_own, fc_there = jnp.where(first, sums[FC, 0], sums[FC, 1]), swap(fc_away, SECTION)
    sent[QKV, 0], coming = tied(sent[QKV, 0], coming)
    ready[QKV, 0] = add((QKV, 0), None)
    sums[QKV, 0] = scatter_wt(after(ready[QKV, 0], sums[FC, 0]))
    fc_halves = (jnp.where(first, fc_own, fc_there), jnp.where(first, fc_there, fc_own))
    fc_parts = [gathered(value, CTX) for value in fc_halves]
    leaving = state([coming], [fc_there])
    sums[PROJ, 0] = scatter_wt(after(ready[PROJ, 0], sums[QKV, 0]))

    def packed(grads):
        def placed(piece):
            zeros = jnp.zeros((plan.padded,), jnp.float32)
            return lax.dynamic_update_slice_in_dim(zeros, piece, ci * plan.step, 0)[:width]

        full = jnp.stack(
            [
                grads["attn_gain"],
                grads["attn_shift"],
                placed(grads["qkv"][:span]),
                placed(grads["qkv"][2 * span :]),
                grads["proj"],
                grads["mlp_gain"],
                grads["mlp_shift"],
                grads["out"],
            ]
        )
        full = jnp.swapaxes(full.reshape(8, owners, shard), 0, 1).reshape(owners, 8 * shard)
        halves = [piece.reshape(owners, half) for piece in grads["fc"]]
        halves = jnp.where(
            first, jnp.concatenate(halves, 1), jnp.concatenate(halves[::-1], 1)
        )
        zeros = jnp.zeros((owners, hidden_rows), jnp.float32)
        return jnp.concatenate(
            [full, lax.dynamic_update_slice_in_dim(zeros, halves, ci * part, 1)], 1
        )

    late, early = packed(vector_grads[0]), packed(vector_grads[1])
    early = after(early, leaving)
    total = jnp.where(first, late, early) + swap(jnp.where(first, early, late), SECTION)
    for bit in bits_of(CTX):
        total = total + swap(total, CTX, bit)
    pieces = {
        at: lax.dynamic_index_in_dim(total, plan.wi ^ at, 0, keepdims=False) for at in range(owners)
    }
    for bit in bits_of(WT):
        for at in sorted(pieces, reverse=True):
            if at & bit:
                pieces[at ^ bit] = pieces[at ^ bit] + swap(pieces.pop(at), WT, bit)
    total = pieces[0]
    vector_out = total[: 8 * shard].reshape(8, shard)
    fc_bias_out = total[8 * shard :]

    stays = jnp.where(first, coming, leaving)
    came = swap(jnp.where(first, leaving, coming), SECTION)
    result = jnp.where(first, jnp.stack([stays, came]), jnp.stack([came, stays]))
    result = result.reshape(1, 2, 1, rows, width)
    result = after(result, *jax.tree.leaves(started))
    out_grad = joined_rows(owned[OUT], ci)
    segments = [
        (kind, owner, at * half, at * hidden_rows + owner * part + kind * half, half)
        for at in range(owners)
        for owner in range(count)
        for kind in range(2)
    ]
    fc_grad = joined_columns(fc_parts, segments, ci, owners * hidden_rows)
    qkv_own, qkv_there = to_owner(QKV)
    qkv_halves = [jnp.where(first, qkv_own, qkv_there), jnp.where(first, qkv_there, qkv_own)]
    qkv_parts = gathered(jnp.concatenate(qkv_halves), CTX)
    segments = [
        (
            0,
            owner,
            at * span,
            at * width + owner * plan.step,
            plan.step if owner < count - 1 else width - plan.step * (count - 1),
        )
        for at in range(3)
        for owner in range(count)
    ]
    qkv_grad = joined_columns([qkv_parts], segments, ci, 3 * width)
    proj_own, proj_there = to_owner(PROJ)
    proj_parts = gathered(low(wide(proj_own) + wide(proj_there)), CTX)
    starts = [plan.proj_start(ci ^ at) for at in range(count)]
    proj_grad = placed_rows(proj_parts, starts, 1, shard, jnp.float32)

    return (
        result,
        vector_out[0][None],
        vector_out[1][None],
        qkv_grad[None],
        vector_out[2][None],
        vector_out[3][None],
        proj_grad[None],
        vector_out[4][None],
        vector_out[5][None],
        vector_out[6][None],
        fc_grad[None],
        fc_bias_out[None],
        out_grad[None],
        vector_out[7][None],
    )


def solution(mesh):
    return jax.shard_map(
        body,
        mesh=mesh,
        in_specs=(
            P(SECTION, None, WT, CTX, None),
            P(),
            P(SECTION, WT),
            P(SECTION, WT),
            P(SECTION, WT, None),
            P(SECTION, WT),
            P(SECTION, WT),
            P(SECTION, WT, None),
            P(SECTION, WT),
            P(SECTION, WT),
            P(SECTION, WT),
            P(SECTION, WT, None),
            P(SECTION, WT),
            P(SECTION, WT, None),
            P(SECTION, WT),
        ),
        out_specs=(
            P(SECTION, None, WT, CTX, None),
            P(SECTION, WT),
            P(SECTION, WT),
            P(SECTION, WT, None),
            P(SECTION, WT),
            P(SECTION, WT),
            P(SECTION, WT, None),
            P(SECTION, WT),
            P(SECTION, WT),
            P(SECTION, WT),
            P(SECTION, WT, None),
            P(SECTION, WT),
            P(SECTION, WT, None),
            P(SECTION, WT),
        ),
        check_vma=False,
    )
```

```python
import functools
import math

import jax
import jax.numpy as jnp
from jax import lax
from jax.experimental import pallas as pl
from jax.experimental.pallas import tpu as pltpu
from jax.sharding import PartitionSpec as P

SECTION, CTX, WT = "section", "ctx", "wt"
QKV, PROJ, FC, OUT = range(4)
OWN, NORM, SCORES, MIXED, GATHERED, ACTIVE, RESULT = range(7)
START, HIDDEN, SECOND, SUM, HEADS, BACK, THERE, FIRST, END = range(9)
FULL, MOVED, SEND, CAME, REDUCE, DONE, HOP, OWNED, TOKEN = range(9)

HEAD_DIM = 64
NEG = -1000000000.0
LANES = 128


def nt_dot(left, right):
    return lax.dot_general(left, right, (((1,), (1,)), ((), ())), preferred_element_type=jnp.float32)


def nn_dot(left, right):
    return jnp.dot(left, right, preferred_element_type=jnp.float32)


def causal_scores(keys, query, tile):
    scores = nt_dot(keys, query)
    edge = scores.shape[0] - tile
    key_at = lax.broadcasted_iota(jnp.int32, (tile, tile), 0)
    query_at = lax.broadcasted_iota(jnp.int32, (tile, tile), 1)
    last = jnp.where(key_at <= query_at, scores[edge:], NEG)
    return jnp.concatenate([scores[:edge], last], 0) if edge else last


def attend_kernel(block, tile, heads, place, qkv, out, log_total, query, keyed, valued, mixed):
    length, three = qkv.shape
    span = three // 3
    lane = lax.broadcasted_iota(jnp.int32, (tile, LANES), 1)

    def pair(index, carry):
        start = pl.multiple_of(index * LANES, LANES)
        for at in range(length // block):
            rows = pl.ds(pl.multiple_of(place[at] * block, block), block)
            here = pl.ds(at * block, block)
            query[here, :] = qkv[rows, pl.ds(start, LANES)] * (HEAD_DIM ** (-0.5))
            keyed[here, :] = qkv[rows, pl.ds(span + start, LANES)]
            valued[:, here] = qkv[rows, pl.ds(2 * span + start, LANES)].T

        for half in range(2):

            @pl.when(2 * index + half < heads)
            def _():
                mine = (lane < HEAD_DIM) if half == 0 else (lane >= HEAD_DIM)
                features = slice(half * HEAD_DIM, (half + 1) * HEAD_DIM)
                for at in range(length // tile):
                    seen = (at + 1) * tile
                    cols = slice(at * tile, seen)
                    part = jnp.where(mine, query[cols, :], 0)
                    scores = causal_scores(keyed[:seen, :], part, tile)
                    highest = jnp.max(scores, 0, keepdims=True)
                    exponent = jnp.exp(scores - highest)
                    total = jnp.sum(exponent, 0, keepdims=True)
                    result = nn_dot(valued[features, :seen], exponent.astype(jnp.bfloat16))
                    mixed[features, cols] = result * (1.0 / total)
                    log_total[pl.ds(2 * index + half, 1), cols] = highest + jnp.log(total)

        for at in range(length // block):
            rows = pl.ds(pl.multiple_of(place[at] * block, block), block)
            out[rows, pl.ds(start, LANES)] = mixed[:, at * block : (at + 1) * block].T.astype(out.dtype)
        return carry

    mixed[...] = jnp.zeros_like(mixed)
    lax.fori_loop(0, span // LANES, pair, 0)


def attend(place, qkv, heads, block):
    length, three = qkv.shape
    span = three // 3
    tile = min(256, length)
    rows = -(-span // HEAD_DIM // 8) * 8
    vmem = pl.BlockSpec(memory_space=pltpu.VMEM)
    return pl.pallas_call(
        functools.partial(attend_kernel, block, tile, heads),
        out_shape=(
            jax.ShapeDtypeStruct((length, span), jnp.bfloat16),
            jax.ShapeDtypeStruct((rows, length), jnp.float32),
        ),
        in_specs=[pl.BlockSpec(memory_space=pltpu.SMEM), vmem],
        out_specs=(vmem, vmem),
        scratch_shapes=[
            pltpu.VMEM((length, LANES), jnp.bfloat16),
            pltpu.VMEM((length, LANES), jnp.bfloat16),
            pltpu.VMEM((LANES, length), jnp.bfloat16),
            pltpu.VMEM((LANES, length), jnp.float32),
        ],
        compiler_params=pltpu.CompilerParams(vmem_limit_bytes=40 * 1024 * 1024),
        cost_estimate=pl.CostEstimate(
            flops=0, bytes_accessed=0, transcendentals=0
        ),
    )(place, qkv)


def attend_back_kernel(
    block, tile, heads, place, qkv, grad_mixed, log_total, out,
    query, keyed, keyed_t, valued, grad, grad_query, grad_key, grad_value,
):
    length, three = qkv.shape
    span = three // 3
    scale = HEAD_DIM ** (-0.5)
    lane = lax.broadcasted_iota(jnp.int32, (tile, LANES), 1)

    def pair(index, carry):
        start = pl.multiple_of(index * LANES, LANES)
        for at in range(length // block):
            rows = pl.ds(pl.multiple_of(place[at] * block, block), block)
            here = pl.ds(at * block, block)
            query[here, :] = qkv[rows, pl.ds(start, LANES)] * scale
            key_part = qkv[rows, pl.ds(span + start, LANES)]
            keyed[here, :] = key_part
            keyed_t[:, here] = key_part.T
            valued[here, :] = qkv[rows, pl.ds(2 * span + start, LANES)]
            grad[here, :] = grad_mixed[rows, pl.ds(start, LANES)]
        grad_query[...] = jnp.zeros_like(grad_query)
        grad_key[...] = jnp.zeros_like(grad_key)
        grad_value[...] = jnp.zeros_like(grad_value)

        for half in range(2):

            @pl.when(2 * index + half < heads)
            def _():
                mine = (lane < HEAD_DIM) if half == 0 else (lane >= HEAD_DIM)
                features = slice(half * HEAD_DIM, (half + 1) * HEAD_DIM)
                for at in range(length // tile):
                    seen = (at + 1) * tile
                    cols = slice(at * tile, seen)
                    part = jnp.where(mine, query[cols, :], 0)
                    grad_part = jnp.where(mine, grad[cols, :], 0)
                    scores = causal_scores(keyed[:seen, :], part, tile)
                    chance = jnp.exp(scores - log_total[pl.ds(2 * index + half, 1), cols])
                    grad_chance = nt_dot(valued[:seen, :], grad_part)
                    inner = jnp.sum(chance * grad_chance, 0, keepdims=True)
                    grad_scores = (chance * (grad_chance - inner)).astype(jnp.bfloat16)
                    grad_value[:seen, :] += nn_dot(chance.astype(jnp.bfloat16), grad_part)
                    grad_key[:seen, :] += nn_dot(grad_scores, part)
                    grad_query[features, cols] = nn_dot(keyed_t[features, :seen], grad_scores) * scale

        for at in range(length // block):
            rows = pl.ds(pl.multiple_of(place[at] * block, block), block)
            here = slice(at * block, (at + 1) * block)
            out[rows, pl.ds(start, LANES)] = grad_query[:, here].T.astype(out.dtype)
            out[rows, pl.ds(span + start, LANES)] = grad_key[here, :].astype(out.dtype)
            out[rows, pl.ds(2 * span + start, LANES)] = grad_value[here, :].astype(out.dtype)
        return carry

    lax.fori_loop(0, span // LANES, pair, 0)


def attend_back(place, qkv, grad_mixed, log_total, heads, block):
    length, three = qkv.shape
    span = three // 3
    tile = min(256, length)
    vmem = pl.BlockSpec(memory_space=pltpu.VMEM)
    return pl.pallas_call(
        functools.partial(attend_back_kernel, block, tile, heads),
        out_shape=jax.ShapeDtypeStruct((length, three), jnp.bfloat16),
        in_specs=[pl.BlockSpec(memory_space=pltpu.SMEM), vmem, vmem, vmem],
        out_specs=vmem,
        scratch_shapes=[
            pltpu.VMEM((length, LANES), jnp.bfloat16),
            pltpu.VMEM((length, LANES), jnp.bfloat16),
            pltpu.VMEM((LANES, length), jnp.bfloat16),
            pltpu.VMEM((length, LANES), jnp.bfloat16),
            pltpu.VMEM((length, LANES), jnp.bfloat16),
            pltpu.VMEM((LANES, length), jnp.float32),
            pltpu.VMEM((length, LANES), jnp.float32),
            pltpu.VMEM((length, LANES), jnp.float32),
        ],
        compiler_params=pltpu.CompilerParams(vmem_limit_bytes=48 * 1024 * 1024),
        cost_estimate=pl.CostEstimate(
            flops=0, bytes_accessed=0, transcendentals=0
        ),
    )(place, qkv, grad_mixed, log_total)


EPS = 1e-05
GELU_A = math.sqrt(2.0 / math.pi)
GELU_B = 0.044715


def flip(axis, bit):
    return [(at, at ^ bit) for at in range(lax.axis_size(axis))]


def swap(value, axis, bit=1):
    return lax.ppermute(value, axis, flip(axis, bit))


def bits_of(axis):
    bits, bit = [], 1
    while bit < lax.axis_size(axis):
        bits.append(bit)
        bit *= 2
    return bits


def gathered(value, axis):
    pieces = {0: value}
    for bit in reversed(bits_of(axis)):
        for at in list(pieces):
            pieces[at | bit] = swap(pieces[at], axis, bit)
    return [pieces[at] for at in range(lax.axis_size(axis))]


def gathered_whole(value, axis):
    pieces = {0: value}
    for bit in reversed(bits_of(axis)):
        held = list(pieces)
        for at, came in zip(held, together([pieces[at] for at in held], axis, bit)):
            pieces[at | bit] = came
    return [pieces[at] for at in range(lax.axis_size(axis))]


def together(pieces, axis, bit):
    if len(pieces) == 1:
        return [swap(pieces[0], axis, bit)]
    came = swap(jnp.concatenate(pieces), axis, bit)
    rows = pieces[0].shape[0]
    return [came[at * rows : (at + 1) * rows] for at in range(len(pieces))]


def summed(pieces, axis, bits=None):
    pieces = dict(pieces) if isinstance(pieces, dict) else dict(enumerate(pieces))
    for bit in bits_of(axis) if bits is None else bits:
        for at in sorted(pieces, reverse=True):
            if at & bit:
                came = swap(pieces.pop(at).astype(jnp.bfloat16), axis, bit)
                pieces[at ^ bit] = pieces[at ^ bit].astype(jnp.float32) + came.astype(jnp.float32)
    return pieces[0] if len(pieces) == 1 else pieces


def exchanged(pieces, axis):
    return [swap(piece, axis, at) if at else piece for at, piece in enumerate(pieces)]


def at_once(go, step, operands, aside=None):
    aside = aside or []
    counts = [len(inputs) for unused, inputs in aside]

    def both(operands, inputs):
        results, at = [], 0
        for (work, unused), count in zip(aside, counts):
            results.append(work(*inputs[at : at + count]))
            at += count
        return step(*operands), results

    inputs = [value for unused, values in aside for value in values]
    shapes = jax.eval_shape(both, operands, inputs)

    def nothing(*unused):
        return jax.tree.map(lambda shape: jnp.zeros(shape.shape, shape.dtype), shapes)

    return lax.cond(go, both, nothing, operands, inputs)


def by_owner(pieces, axis):
    here = lax.axis_index(axis)
    whole = jnp.zeros((len(pieces),) + pieces[0].shape, pieces[0].dtype)
    for at, piece in enumerate(pieces):
        whole = lax.dynamic_update_index_in_dim(whole, piece, here ^ at, 0)
    return whole


def after(value, *marks):
    return lax.optimization_barrier(marks + (value,))[-1]


def tied(*values):
    return lax.optimization_barrier(values)


def over_wt(value, tiled=True):
    return lax.all_gather(value, WT, axis=0, tiled=tiled)


def scatter_wt(value, tiled=True):
    return lax.psum_scatter(value, WT, scatter_dimension=0, tiled=tiled)


def dot(left, right):
    return jnp.dot(left, right, preferred_element_type=jnp.float32)


def dot_nt(left, right):
    return lax.dot_general(left, right, (((1,), (1,)), ((), ())), preferred_element_type=jnp.float32)


def dot_tn(left, right):
    return lax.dot_general(left, right, (((0,), (0,)), ((), ())), preferred_element_type=jnp.float32)


def low(value):
    return value.astype(jnp.bfloat16)


def wide(value):
    return value.astype(jnp.float32)


def normed(values):
    center = values - jnp.mean(values, -1, keepdims=True)
    rate = lax.rsqrt(jnp.mean(center * center, -1, keepdims=True) + EPS)
    return center * rate, rate


def norm_back(grad, gain, values):
    unit, rate = normed(values)
    inner = grad * gain
    back = (
        inner
        - jnp.mean(inner, -1, keepdims=True)
        - unit * jnp.mean(inner * unit, -1, keepdims=True)
    ) * rate
    return back, jnp.sum(grad * unit, 0), jnp.sum(grad, 0)


def gelu(value):
    return 0.5 * value * (1.0 + jnp.tanh(GELU_A * (value + GELU_B * value * value * value)))


def gelu_slope(value):
    square = value * value
    bend = jnp.tanh(GELU_A * (value + GELU_B * value * square))
    return 0.5 * (1.0 + bend) + 0.5 * value * (1.0 - bend * bend) * (
        GELU_A * (1.0 + 3.0 * GELU_B * square)
    )


def joined_kernel(count, segments, at, *refs):
    out, pieces = refs[-1], refs[:-1]
    kinds = len(pieces) // count
    picked = {}
    for kind, owner, source, target, columns in segments:
        if (kind, owner) not in picked:
            value = pieces[kind * count][...].astype(jnp.float32)
            for step in range(1, count):
                other = pieces[kind * count + step][...].astype(jnp.float32)
                value = jnp.where((at[0] ^ owner) == step, other, value)
            picked[kind, owner] = value
        out[:, target : target + columns] = picked[kind, owner][:, source : source + columns]
    assert kinds * count == len(pieces)


def joined_columns(pieces, kinds, segments, ci, columns):
    flat = pieces * kinds
    rows = flat[0].shape[0] // kinds
    tile = 80 if rows % 80 == 0 else rows
    return pl.pallas_call(
        functools.partial(joined_kernel, len(pieces), segments),
        out_shape=jax.ShapeDtypeStruct((rows, columns), jnp.float32),
        grid=(rows // tile,),
        in_specs=[pl.BlockSpec(memory_space=pltpu.SMEM)]
        + [
            pl.BlockSpec((tile, piece.shape[1]), lambda at, kind=kind: (kind * (rows // tile) + at, 0))
            for kind in range(kinds)
            for piece in pieces
        ],
        out_specs=pl.BlockSpec((tile, columns), lambda at: (at, 0)),
        compiler_params=pltpu.CompilerParams(vmem_limit_bytes=48 * 1024 * 1024),
        cost_estimate=pl.CostEstimate(
            flops=0, bytes_accessed=6 * rows * columns, transcendentals=0
        ),
    )(ci.reshape(1), *flat)


class Plan:
    def __init__(self, width, hidden_rows, go):
        self.go = go
        self.count = lax.axis_size(CTX)
        self.ci = lax.axis_index(CTX)
        self.first = lax.axis_index(SECTION) == 0
        self.xi = lax.axis_index(SECTION)
        self.wi = lax.axis_index(WT)
        self.width = width
        heads = width // HEAD_DIM
        stride = heads // self.count
        self.heads = heads - stride * (self.count - 1)
        self.step = stride * HEAD_DIM
        self.span = (self.heads + self.heads % 2) * HEAD_DIM
        self.padded = self.step * (self.count - 1) + self.span
        self.owned = jnp.where(self.ci == self.count - 1, self.heads, stride) * HEAD_DIM
        self.part = hidden_rows // self.count
        self.half = self.part // 2
        self.shard = width // lax.axis_size(WT)
        self.proj_rows = -(-self.shard // self.count // 16) * 16

    def proj_start(self, index):
        return jnp.minimum(index * self.proj_rows, self.shard - self.proj_rows)

    def gathered(self, value):
        def step(value):
            return gathered(value, CTX)[1:]

        return [value] + at_once(self.go, step, [value])[0]

    def exchanged(self, pieces, aside=None):
        def step(*pieces):
            return [swap(piece, CTX, at + 1) for at, piece in enumerate(pieces)]

        came, extra = at_once(self.go, step, pieces[1:], aside)
        return pieces[:1] + came, extra

    def summed(self, value, aside=None):
        def step(value):
            return wide(summed(cut(value, self.count), CTX))

        return at_once(self.go, step, [value], aside)

    def proj_parts(self, left, right):
        parts = grad_dot(left, right).reshape(-1, self.shard, self.width)
        return [
            lax.dynamic_slice_in_dim(parts, self.proj_start(self.ci ^ at), self.proj_rows, 1)
            for at in range(self.count)
        ]

    def padded_out(self, array):
        return jnp.pad(array, [(0, 0)] * (array.ndim - 1) + [(0, self.padded - array.shape[-1])])

    def window(self, padded, index):
        return lax.dynamic_slice_in_dim(padded, index * self.step, self.span, padded.ndim - 1)

    def joined(self, ordered):
        last = self.width - self.step * (self.count - 1)
        parts = [ordered[at, ..., : self.step] for at in range(self.count - 1)]
        return jnp.concatenate(parts + [ordered[self.count - 1, ..., :last]], -1)


def joined_rows_kernel(at, *refs):
    out, pieces = refs[-1], refs[:-1]
    step = pl.program_id(0)
    for index, piece in enumerate(pieces):

        @pl.when(step == index)
        def _():
            out[...] = piece[...].astype(jnp.float32)


def joined_rows(pieces, ci):
    rows, columns = pieces[0].shape
    count = len(pieces)
    if rows % 8:
        return wide(by_owner(pieces, CTX)).reshape(count * rows, columns)
    return pl.pallas_call(
        joined_rows_kernel,
        out_shape=jax.ShapeDtypeStruct((count * rows, columns), jnp.float32),
        grid_spec=pltpu.PrefetchScalarGridSpec(
            num_scalar_prefetch=1,
            grid=(count,),
            in_specs=[pl.BlockSpec((rows, columns), lambda step, at: (0, 0))] * count,
            out_specs=pl.BlockSpec((rows, columns), lambda step, at: (at[0] ^ step, 0)),
        ),
        compiler_params=pltpu.CompilerParams(vmem_limit_bytes=48 * 1024 * 1024),
        cost_estimate=pl.CostEstimate(
            flops=0, bytes_accessed=6 * count * rows * columns, transcendentals=0
        ),
    )(ci.reshape(1), *pieces)


def placed_kernel(owners, start, *refs):
    out, pieces = refs[-1], refs[:-1]
    rows = pieces[0].shape[0] // owners
    shard = out.shape[0] // owners
    for at, piece in enumerate(pieces):
        for owner in range(owners):
            here = pl.ds(pl.multiple_of(owner * shard + start[at], 16), rows)
            out[here, :] = piece[owner * rows : (owner + 1) * rows, :].astype(out.dtype)


def placed_rows(pieces, starts, owners, shard, dtype):
    columns = pieces[0].shape[1]
    vmem = pl.BlockSpec(memory_space=pltpu.VMEM)
    return pl.pallas_call(
        functools.partial(placed_kernel, owners),
        out_shape=jax.ShapeDtypeStruct((owners * shard, columns), dtype),
        in_specs=[pl.BlockSpec(memory_space=pltpu.SMEM)] + [vmem] * len(pieces),
        out_specs=vmem,
        compiler_params=pltpu.CompilerParams(vmem_limit_bytes=48 * 1024 * 1024),
        cost_estimate=pl.CostEstimate(
            flops=0, bytes_accessed=4 * owners * shard * columns, transcendentals=0
        ),
    )(jnp.stack(starts), *pieces)


def cut(value, count):
    rows = value.shape[0] // count
    return [value[at * rows : (at + 1) * rows] for at in range(count)]


def forward_layer(entering, weight, vectors, plan, place, block, pin):
    attn_gain, attn_shift, bias_qkv, proj_bias, mlp_gain, mlp_shift, fc_bias, out_bias = vectors
    stream = wide(entering)
    first_norm = pin(OWN, low(normed(stream)[0] * attn_gain + attn_shift))
    first_norm = jnp.concatenate(pin(NORM, plan.gathered(first_norm)))
    qkv = pin(SCORES, low(dot(first_norm, weight(QKV)) + bias_qkv))
    mixed, log_total = attend(place, qkv, plan.heads, block)
    mixed = pin(MIXED, mixed)
    mixed_all = plan.joined(by_owner(plan.exchanged(cut(mixed, plan.count))[0], CTX))
    middle = (dot(mixed_all, weight(PROJ)) + proj_bias) + stream
    second_norm = low(normed(middle)[0] * mlp_gain + mlp_shift)
    second_norm = jnp.concatenate(pin(GATHERED, plan.gathered(second_norm)))
    hidden = [dot(second_norm, part) + bias for part, bias in zip(weight(FC), fc_bias)]
    active = pin(ACTIVE, [low(gelu(part)) for part in hidden])

    def final(first_marks=(), last_marks=()):
        parts = after(active, *first_marks)
        w_out = weight(OUT)
        result = pin(RESULT, low(dot(parts[0], w_out[0]) + dot(parts[1], w_out[1])))
        return low((plan.summed(after(result, *last_marks))[0] + out_bias) + middle)

    kept = (stream, first_norm, qkv, log_total, mixed_all, middle, second_norm, hidden, active)
    return final, kept


def grad_dot(left, right):
    return low(dot_tn(left, right))


def grad_dot_all(left, *right):
    return low(dot_tn(left, jnp.concatenate(right)))


def backward_layer(coming, coming_all, kept, weight, vectors, plan, place, block, pin, aside):
    attn_gain, attn_shift, bias_qkv, proj_bias, mlp_gain, mlp_shift, fc_bias, out_bias = vectors
    stream, first_norm, qkv, log_total, mixed_all, middle, second_norm, hidden, active = kept
    grads, sums = {}, {}
    w_fc, w_out = weight(FC), weight(OUT)
    grads[OUT] = [(grad_dot_all, [part] + coming_all) for part in active]
    coming_all = pin(START, coming_all, grads)
    grads[OUT] = [(grad_dot_all, [part] + coming_all) for part in active]
    coming_whole = jnp.concatenate(coming_all)
    grad_hidden = [
        low(dot_nt(coming_whole, part) * gelu_slope(at)) for part, at in zip(w_out, hidden)
    ]
    grads[FC] = [(grad_dot, [second_norm, part]) for part in grad_hidden]
    grad_hidden = pin(HIDDEN, grad_hidden, grads)
    grads[FC] = [(grad_dot, [second_norm, part]) for part in grad_hidden]
    grad_second = low(dot_nt(grad_hidden[0], w_fc[0]) + dot_nt(grad_hidden[1], w_fc[1]))
    grad_second = pin(SECOND, grad_second, grads)
    grad_norm = aside(SUM, lambda extra: plan.summed(grad_second, extra), grads)
    grad_norm = pin(SUM, grad_norm, grads)
    back, sums["mlp_gain"], sums["mlp_shift"] = norm_back(grad_norm, mlp_gain, middle)
    grad_final = wide(coming)
    grad_middle = back + grad_final
    branch = low(grad_middle)
    grad_mixed = plan.padded_out(low(dot_nt(branch, weight(PROJ))))
    pieces = [plan.window(grad_mixed, plan.ci ^ at) for at in range(plan.count)]
    grads[PROJ] = [(plan.proj_parts, [mixed_all, branch])]
    grad_heads = aside(HEADS, lambda extra: plan.exchanged(pieces, extra), grads)
    grad_heads = jnp.concatenate(grad_heads)
    column = lax.broadcasted_iota(jnp.int32, grad_heads.shape, 1)
    grad_heads = pin(HEADS, jnp.where(column < plan.owned, grad_heads, 0), grads)
    grad_qkv = attend_back(place, qkv, grad_heads, log_total, plan.heads, block)
    grad_qkv = pin(BACK, grad_qkv, grads)
    grads[QKV] = [(grad_dot, [first_norm, grad_qkv])]
    grad_qkv = pin(THERE, grad_qkv, grads)
    grad_first = pin(FIRST, low(dot_nt(grad_qkv, weight(QKV))), grads)
    grad_norm = aside(END, lambda extra: plan.summed(grad_first, extra), grads)
    grad_norm = pin(END, grad_norm, grads)
    back, sums["attn_gain"], sums["attn_shift"] = norm_back(grad_norm, attn_gain, stream)
    leaving = low(back + grad_middle)
    sums["fc"] = [jnp.sum(wide(part), 0) for part in grad_hidden]
    sums["out"] = jnp.sum(grad_final, 0)
    sums["proj"] = jnp.sum(wide(branch), 0)
    sums["qkv"] = jnp.sum(wide(grad_qkv), 0)
    return leaving, sums


def body(
    feed,
    block_order,
    attn_gain,
    attn_shift,
    w_qkv,
    query_bias,
    value_bias,
    w_proj,
    proj_bias,
    mlp_gain,
    mlp_shift,
    w_fc,
    fc_bias,
    w_out,
    out_bias,
):
    width = w_proj.shape[2]
    shard = w_proj.shape[1]
    hidden_rows = w_out.shape[1]
    plan = Plan(width, hidden_rows, block_order[0] >= 0)
    count, owners = plan.count, lax.axis_size(WT)
    first, xi, ci = plan.first, plan.xi, plan.ci
    part, half, span = plan.part, plan.half, plan.span
    rows = feed.shape[3]
    block = rows // 2

    def mine_other(mine, other):
        return (jnp.where(first, mine, other), jnp.where(first, other, mine))

    slots = jnp.arange(2 * count, dtype=jnp.int32)
    held = 2 * (ci ^ (slots // 2)) + slots % 2
    table = (held[:, None] == slots[None, :]).astype(jnp.int32)
    blocks_held = jnp.sum(table * block_order[None, :], 1)
    found = (blocks_held[None, :] == slots[:, None]).astype(jnp.int32)
    place = jnp.sum(found * slots[None, :], 1)

    fc_part = lax.dynamic_slice_in_dim(fc_bias[0], ci * part, part, 0)
    names = (attn_gain, attn_shift, query_bias, value_bias, proj_bias, mlp_gain, mlp_shift, out_bias)
    small = jnp.concatenate([vector[0] for vector in names] + [fc_part])
    local = feed[0, :, 0]
    feed_own = lax.dynamic_index_in_dim(local, xi, 0, keepdims=False)
    feed_gone = lax.dynamic_index_in_dim(local, 1 - xi, 0, keepdims=False)

    def fc_shard(duty):
        return jnp.concatenate(
            [
                lax.dynamic_slice_in_dim(
                    w_fc[0], owner * hidden_rows + ci * part + duty * half, half, 1
                )
                for owner in range(owners)
            ],
            1,
        )

    def out_shard(duty):
        return lax.dynamic_slice_in_dim(w_out[0], ci * part + duty * half, half, 0)

    qkv_shard = jnp.concatenate(
        [
            plan.window(plan.padded_out(w_qkv[0][:, at * width : (at + 1) * width]), ci)
            for at in range(3)
        ],
        1,
    )
    proj_shard = lax.dynamic_slice_in_dim(w_proj[0], plan.proj_start(ci), plan.proj_rows, 0)

    def qkv_half(duty):
        return lax.dynamic_slice_in_dim(qkv_shard, duty * (shard // 2), shard // 2, 0)

    whole_here = {(OUT, 1)}
    own_shards = {QKV: qkv_half(xi), PROJ: proj_shard, FC: fc_shard(xi), OUT: out_shard(xi)}
    gone = {QKV: qkv_half(1 - xi), PROJ: proj_shard, FC: fc_shard(1 - xi), OUT: out_shard(1 - xi)}
    came = {QKV: swap(gone[QKV], SECTION)}
    started = [came[QKV]]
    feed_gone = after(feed_gone, gone[QKV])
    feed_came = swap(feed_gone, SECTION)
    small_came = swap(after(small, feed_gone), SECTION)
    started += [feed_came, small_came]
    before = feed_gone
    for name in (PROJ, FC, OUT):
        before = after(gone[name], before)
        came[name] = swap(before, SECTION)
        started.append(came[name])
    shards = {name: mine_other(own_shards[name], came[name]) for name in (QKV, PROJ)}
    last_gone = after(own_shards[OUT], before)
    last_came = swap(last_gone, SECTION)

    entering, coming = mine_other(feed_own, feed_came)
    small = jnp.stack(mine_other(small, small_came))
    small = wide(by_owner(gathered(small, WT), WT))

    def vectors_of(layer):
        full = jnp.swapaxes(small[:, layer, : 8 * shard].reshape(owners, 8, shard), 0, 1)
        full = full.reshape(8, owners * shard)
        hidden = small[:, layer, 8 * shard :]
        halves = [
            lax.dynamic_slice_in_dim(hidden, duty * half, half, 1).reshape(-1) for duty in (xi, 1 - xi)
        ]
        query = plan.window(plan.padded_out(full[2]), ci)
        value = plan.window(plan.padded_out(full[3]), ci)
        bias_qkv = jnp.concatenate([query, jnp.zeros_like(query), value])
        return (full[0], full[1], bias_qkv, full[4], full[5], full[6], halves, full[7])

    vectors = [vectors_of(layer) for layer in range(2)]
    full, operands = {}, []
    tiny = small_came[:128]

    def gather_over_wt(keys, *marks):
        for key in keys:
            name, layer = key
            piece = after(shards[name][layer], *operands[-1:], *marks)
            operands.append(piece)
            full[key] = over_wt(piece)
            started.append(full[key])

    gather_over_wt([(QKV, 0)])
    gather_over_wt([(PROJ, 0)], feed_came, small_came)

    made, moved = {}, {}

    def move(key):
        if key not in moved:
            value = full[key]
            if key[0] == PROJ:
                moved[key] = gathered(value, CTX)
            elif key in whole_here:
                moved[key] = None
            else:
                moved[key] = swap(value, SECTION)
            started.append(moved[key])
        return moved[key]

    def weight(layer, name):
        key = (name, layer)
        if key in made:
            return made[key]
        other, value = move(key), full[key]
        if name == QKV:
            halves = [part.reshape(owners, shard // 2, 3 * span) for part in mine_other(value, other)]
            result = jnp.stack(halves, 1).reshape(width, 3 * span)
        elif name == PROJ:
            starts = [plan.proj_start(ci ^ at) for at in range(count)]
            result = placed_rows(other, starts, owners, shard, jnp.bfloat16)
        elif key in whole_here:
            result = tuple(value[:, at].reshape(-1, value.shape[-1]) for at in range(2))
        else:
            result = (value, other)
        made[key] = result
        return result

    front = {
        (0, OWN): ((FULL, QKV, 0),),
        (0, NORM): ((FULL, PROJ, 0),),
        (0, MIXED): ((MOVED, PROJ, 0), (FULL, FC, 0)),
        (0, GATHERED): ((MOVED, FC, 0), (FULL, OUT, 0)),
        (0, ACTIVE): ((FULL, PROJ, 1),),
        (0, RESULT): ((MOVED, PROJ, 1), (FULL, QKV, 1)),
        (1, NORM): ((MOVED, QKV, 1), (FULL, FC, 1), (TOKEN,)),
        (1, GATHERED): ((MOVED, FC, 1),),
    }

    coming_parts = []

    def forward_pin(layer):
        def pin(point, value):
            if (layer, point) == (0, OWN):
                for name in (FC, OUT):
                    shards[name] = mine_other(own_shards[name], after(came[name], value))
                keys = [(FC, 0), (OUT, 0), (PROJ, 1), (QKV, 1), (FC, 1)]
                gather_over_wt(keys, value)
            if (layer, point) == (0, MIXED):
                last, value = tied(last_came, value)
                shards[OUT, 1] = jnp.stack([shards[OUT][1], mine_other(gone[OUT], last)[1]])
            if (layer, point) == (0, ACTIVE):
                piece, value = tied(shards[OUT, 1], value)
                full[OUT, 1] = over_wt(after(piece, operands[-1]), tiled=False)
                started.append(full[OUT, 1])
            for kind, *key in front.get((layer, point), ()):
                key = tuple(key)
                if kind == TOKEN:
                    token, value = tied(tiny, value)
                    token, value = tied(swap(token, CTX), value)
                    started.append(token)
                elif kind == FULL:
                    full[key], value = tied(full[key], value)
                    move(key)
                else:
                    moved[key], value = tied(moved[key], value)
            if (layer, point) == (1, GATHERED):
                coming_parts.extend(gathered(after(coming, *value), CTX))
            return value

        return pin

    kept = []
    state = entering
    for layer in range(2):
        state, kept_here = forward_layer(
            state,
            functools.partial(weight, layer),
            vectors[layer],
            plan,
            place,
            block,
            forward_pin(layer),
        )
        kept.append(kept_here)
        if layer == 0:
            state = state()

    whole_sums = {(OUT, 1)}
    dots, sent, ready, sums, hops, order = {}, {}, {}, {}, {}, []

    def grad_of(key, at, grads):
        if (key, at) not in dots:
            work, inputs = grads[key[0]][at]
            dots[key, at] = work(*inputs)
        return dots[key, at]

    def prepared(key, grads):
        if key[0] == QKV:
            parts = grad_of(key, 0, grads).reshape(owners, 2, shard // 2, 3 * span)
            mine, away = (
                lax.dynamic_index_in_dim(parts, at, 1, keepdims=False).reshape(-1, 3 * span)
                for at in (xi, 1 - xi)
            )
            dots[key, QKV] = mine
            return away
        if key[0] == PROJ:
            return grad_of(key, 0, grads)
        if key in whole_sums:
            halves = [grad_of(key, at, grads).reshape(owners, half, width) for at in range(2)]
            return jnp.stack(halves, 1).reshape(-1, width)
        return grad_of(key, 1, grads)

    def core(*parts):
        return summed(parts, CTX, bits_of(CTX)[:-1])

    def start(key, away):
        if key[0] == PROJ:
            sent[key] = summed(away, CTX, bits_of(CTX)[-1:])
        elif key in whole_sums:
            sent[key] = away
        else:
            sent[key] = swap(away, SECTION)
        started.append(sent[key])

    def add(key, grads):
        came = sent[key]
        if key[0] == PROJ:
            return low(came).reshape(-1, width)
        if key in whole_sums:
            return came
        mine = dots[key, QKV] if key[0] == QKV else grad_of(key, 0, grads)
        return low(wide(came) + wide(mine))

    def hop(key):
        if key not in hops:
            hops[key] = lax.ppermute(sums[key], SECTION, [(1 - key[1], key[1])])
            started.append(hops[key])
        return hops[key]

    def both_halves(key):
        value, came = sums[key], hop(key)
        rows = value.shape[0]
        if key in whole_sums:
            rows = rows // 2
            own = low(wide(value[:rows]) + wide(came[rows:]))
            came = low(wide(value[rows:]) + wide(came[:rows]))
            value = own
        return (value, came) if key[1] == 0 else (came, value)

    def ordered(name):
        late, early = both_halves((name, 0)), both_halves((name, 1))
        return tuple(jnp.where(first, a, b) for a, b in zip(late, early))

    owned = {}
    back = {
        (1, START): ((SEND, OUT, 1), (CAME, OUT, 1), (REDUCE, OUT, 1)),
        (1, HIDDEN): ((SEND, FC, 1),),
        (1, HEADS): ((CAME, FC, 1), (SEND, PROJ, 1), (TOKEN,)),
        (1, BACK): ((DONE, OUT, 1), (REDUCE, FC, 1)),
        (1, FIRST): ((CAME, PROJ, 1),),
        (1, END): ((HOP, OUT, 1), (REDUCE, PROJ, 1), (SEND, QKV, 1), (TOKEN,)),
        (0, START): ((DONE, FC, 1), (SEND, OUT, 0)),
        (0, HIDDEN): ((CAME, QKV, 1),),
        (0, SECOND): ((REDUCE, QKV, 1),),
        (0, SUM): ((CAME, OUT, 0), (SEND, FC, 0), (TOKEN,), (DONE, PROJ, 1)),
        (0, HEADS): ((REDUCE, OUT, 0), (SEND, PROJ, 0), (TOKEN,)),
        (0, BACK): ((DONE, QKV, 1), (DONE, OUT, 0), (CAME, FC, 0), (REDUCE, FC, 0)),
        (0, THERE): ((SEND, QKV, 0), (TOKEN,), (HOP, OUT, 0)),
        (0, FIRST): ((CAME, PROJ, 0), (OWNED, OUT, 0)),
    }
    beside = {
        (1, HEADS): ((PROJ, 0),),
        (1, END): ((QKV, 0),),
        (0, SUM): ((OUT, 0),),
        (0, HEADS): ((PROJ, 0),),
    }

    def backward_pin(layer):
        def pin(point, value, grads):
            for kind, *key in back.get((layer, point), ()):
                key = tuple(key)
                if kind == SEND:
                    away = prepared(key, grads)
                    if key[0] == PROJ:
                        away = at_once(plan.go, core, away)[0]
                    away, value = tied(away, value)
                    start(key, away)
                elif kind == CAME:
                    sent[key], value = tied(sent[key], value)
                    ready[key] = add(key, grads if key[1] == layer else all_grads[key[1]])
                elif kind == TOKEN:
                    token, value = tied(tiny, value)
                    token, value = tied(swap(token, CTX), value)
                    started.append(token)
                elif kind == OWNED:
                    whole, value = tied(jnp.concatenate(ordered(key[0])), value)
                    owned[key[0]] = gathered_whole(whole, CTX)
                elif kind == HOP:
                    hops[key], value = tied(hop(key), value)
                elif kind == DONE:
                    sums[key], value = tied(sums[key], value)
                elif kind == REDUCE:
                    if order:
                        ready[key] = after(ready[key], ready[order[-1]])
                    order.append(key)
                    sums[key] = scatter_wt(ready[key])
                    started.append(sums[key])
            all_grads[layer] = grads
            return value

        return pin

    def beside_of(layer):
        def aside(point, step, grads):
            wanted = beside.get((layer, point), ())
            value, extra = step([grads[name][at] for name, at in wanted])
            for (name, at), result in zip(wanted, extra):
                dots[(name, layer), at] = result
            return value

        return aside

    all_grads = {}
    vector_grads = [None, None]
    for layer in (1, 0):
        coming, vector_grads[layer] = backward_layer(
            coming,
            coming_parts if layer else plan.gathered(coming),
            kept[layer],
            functools.partial(weight, layer),
            vectors[layer],
            plan,
            place,
            block,
            backward_pin(layer),
            beside_of(layer),
        )

    def to_owner(name):
        there = swap(jnp.where(first, sums[name, 1], sums[name, 0]), SECTION)
        return jnp.where(first, sums[name, 0], sums[name, 1]), there

    fc_away, coming = tied(jnp.where(first, sums[FC, 1], sums[FC, 0]), coming)
    fc_own, fc_there = jnp.where(first, sums[FC, 0], sums[FC, 1]), swap(fc_away, SECTION)
    sent[QKV, 0], coming = tied(sent[QKV, 0], coming)
    ready[QKV, 0] = add((QKV, 0), None)
    sums[QKV, 0] = scatter_wt(after(ready[QKV, 0], sums[FC, 0]))
    fc_halves = (jnp.where(first, fc_own, fc_there), jnp.where(first, fc_there, fc_own))
    fc_parts = gathered(jnp.concatenate(fc_halves), CTX)
    leaving = state([coming], [fc_there])
    sums[PROJ, 0] = scatter_wt(after(ready[PROJ, 0], sums[QKV, 0]))

    def packed(grads):
        def placed(piece):
            zeros = jnp.zeros((plan.padded,), jnp.float32)
            return lax.dynamic_update_slice_in_dim(zeros, piece, ci * plan.step, 0)[:width]

        full = jnp.stack(
            [
                grads["attn_gain"],
                grads["attn_shift"],
                placed(grads["qkv"][:span]),
                placed(grads["qkv"][2 * span :]),
                grads["proj"],
                grads["mlp_gain"],
                grads["mlp_shift"],
                grads["out"],
            ]
        )
        full = jnp.swapaxes(full.reshape(8, owners, shard), 0, 1).reshape(owners, 8 * shard)
        halves = [piece.reshape(owners, half) for piece in grads["fc"]]
        halves = jnp.where(
            first, jnp.concatenate(halves, 1), jnp.concatenate(halves[::-1], 1)
        )
        zeros = jnp.zeros((owners, hidden_rows), jnp.float32)
        return jnp.concatenate(
            [full, lax.dynamic_update_slice_in_dim(zeros, halves, ci * part, 1)], 1
        )

    late, early = packed(vector_grads[0]), packed(vector_grads[1])
    early = after(early, leaving)
    total = jnp.where(first, late, early) + swap(jnp.where(first, early, late), SECTION)
    for bit in bits_of(CTX):
        total = total + swap(total, CTX, bit)
    pieces = {
        at: lax.dynamic_index_in_dim(total, plan.wi ^ at, 0, keepdims=False) for at in range(owners)
    }
    for bit in bits_of(WT):
        for at in sorted(pieces, reverse=True):
            if at & bit:
                pieces[at ^ bit] = pieces[at ^ bit] + swap(pieces.pop(at), WT, bit)
    total = pieces[0]
    vector_out = total[: 8 * shard].reshape(8, shard)
    fc_bias_out = total[8 * shard :]

    stays = jnp.where(first, coming, leaving)
    came = swap(jnp.where(first, leaving, coming), SECTION)
    result = jnp.where(first, jnp.stack([stays, came]), jnp.stack([came, stays]))
    result = result.reshape(1, 2, 1, rows, width)
    result = after(result, *jax.tree.leaves(started))
    out_grad = joined_rows(owned[OUT], ci)
    segments = [
        (kind, owner, at * half, at * hidden_rows + owner * part + kind * half, half)
        for at in range(owners)
        for owner in range(count)
        for kind in range(2)
    ]
    fc_grad = joined_columns(fc_parts, 2, segments, ci, owners * hidden_rows)
    qkv_own, qkv_there = to_owner(QKV)
    qkv_halves = [jnp.where(first, qkv_own, qkv_there), jnp.where(first, qkv_there, qkv_own)]
    qkv_parts = gathered(jnp.concatenate(qkv_halves), CTX)
    segments = [
        (
            0,
            owner,
            at * span,
            at * width + owner * plan.step,
            plan.step if owner < count - 1 else width - plan.step * (count - 1),
        )
        for at in range(3)
        for owner in range(count)
    ]
    qkv_grad = joined_columns(qkv_parts, 1, segments, ci, 3 * width)
    proj_own, proj_there = to_owner(PROJ)
    proj_parts = gathered(low(wide(proj_own) + wide(proj_there)), CTX)
    starts = [plan.proj_start(ci ^ at) for at in range(count)]
    proj_grad = placed_rows(proj_parts, starts, 1, shard, jnp.float32)

    return (
        result,
        vector_out[0][None],
        vector_out[1][None],
        qkv_grad[None],
        vector_out[2][None],
        vector_out[3][None],
        proj_grad[None],
        vector_out[4][None],
        vector_out[5][None],
        vector_out[6][None],
        fc_grad[None],
        fc_bias_out[None],
        out_grad[None],
        vector_out[7][None],
    )


def solution(mesh):
    return jax.shard_map(
        body,
        mesh=mesh,
        in_specs=(
            P(SECTION, None, WT, CTX, None),
            P(),
            P(SECTION, WT),
            P(SECTION, WT),
            P(SECTION, WT, None),
            P(SECTION, WT),
            P(SECTION, WT),
            P(SECTION, WT, None),
            P(SECTION, WT),
            P(SECTION, WT),
            P(SECTION, WT),
            P(SECTION, WT, None),
            P(SECTION, WT),
            P(SECTION, WT, None),
            P(SECTION, WT),
        ),
        out_specs=(
            P(SECTION, None, WT, CTX, None),
            P(SECTION, WT),
            P(SECTION, WT),
            P(SECTION, WT, None),
            P(SECTION, WT),
            P(SECTION, WT),
            P(SECTION, WT, None),
            P(SECTION, WT),
            P(SECTION, WT),
            P(SECTION, WT),
            P(SECTION, WT, None),
            P(SECTION, WT),
            P(SECTION, WT, None),
            P(SECTION, WT),
        ),
        check_vma=False,
    )
```
